256 devices in a mesh: lon: 64 (over y, x, z_lo), lat: 4 (over z_hi, core).
Axes of the slice: x: 4, y: 4, z: 8 (z_hi: 2, z_lo: 4; z = z_hi * 4 + z_lo), core: 2. Of those that a mesh axis runs over, the one named last changes fastest.
Arguments:
- ocean_field: float32 [32, 256, 8192], P(None, 'lat', 'lon'), may hold values from -6 to 6
- cotangent: bfloat16 [32, 256, 8192], P(None, 'lat', 'lon'), may hold values from -12 to 12
- mix_coarse: float32 [4, 32, 32], replicated, may hold values from -1 to 1
- mix_detail: float32 [3, 32, 32], replicated, may hold values from -1 to 1
- skip_weight: float32 [32, 32], replicated, may hold values from -1 to 1
- bias_vector: float32 [32], replicated, may hold values from -0.5 to 0.5
Outputs:
- activated: bfloat16 [32, 256, 8192], P(None, 'lat', 'lon')
- grad_field: float32 [32, 256, 8192], P(None, 'lat', 'lon')
- grad_mix_coarse: float32 [4, 32, 32], replicated
- grad_mix_detail: float32 [3, 32, 32], replicated
- grad_skip: float32 [32, 32], replicated
- grad_bias: float32 [32], replicated
The draws below stay inside these ranges and needn't reach their ends.
All inputs are finite; a program needn't handle non-finite values.
Results may differ from the reference program's by a relative error of at most 0.001.
Values sent between devices are 32-bit elements; how exact they have to be, the bound alone decides.
No kernel may reach another device: no remote copies, remote signals or barrier semaphores. Data moves between devices by JAX's collectives and lax.ppermute only.
A program may use at most 128 MiB of HBM per device.

```python
import math
import jax
import jax.numpy as jnp
from jax import lax

C = 32
NLAT = 256
NLON = 8192


def draw_cotangent(key, part):
    key = jax.random.fold_in(key, 7)
    first_key = jax.random.fold_in(key, 0)
    lat_ramp = 1.0 + 2.0 * jnp.arange(NLAT, dtype=jnp.float32) / max(NLAT - 1, 1)
    lon_ramp = 1.0 + 2.0 * jnp.arange(NLON, dtype=jnp.float32) / max(NLON - 1, 1)
    scaling = lat_ramp[:, None] * lon_ramp[None, :] / 3.0
    base_draw = jnp.clip(jax.random.normal(first_key, (C, NLAT, NLON), jnp.float32), -4.0, 4.0)
    return jnp.clip(base_draw * scaling, -12.0, 12.0).astype(jnp.bfloat16)


def steps_of(rng, shape, cuts, smallest, largest):
    level, own = 1.0, jax.random.fold_in(rng, 6)
    for axis_at, shards_of in cuts:
        draws = jnp.exp(jax.random.uniform(jax.random.fold_in(own, axis_at), (shards_of,), jnp.float32, smallest / len(cuts), largest / len(cuts)))
        level = level * jnp.repeat(draws, shape[axis_at] // shards_of).reshape([-1 if axis == axis_at else 1 for axis in range(len(shape))])
    return level


def centred(key, shape, scale, limit, cuts=(), kind=jnp.bfloat16):
    level = steps_of(key, shape, cuts, -0.22, 0.18) if cuts else 1.0
    entries = jax.random.normal(key, shape, jnp.float32) * scale * level
    return jnp.minimum(jnp.maximum(entries, -limit), limit).astype(kind)


def setup_inputs(seed: int = 0) -> dict:
    streams_of = jax.random.split(jax.random.key(seed), 7)
    ocean_field = centred(streams_of[0], (C, NLAT, NLON), 1.0, 6.0, ((1, 4), (2, 64)), jnp.float32)
    cotangent = draw_cotangent(jax.random.fold_in(streams_of[6], 71), 0)
    mix_coarse = centred(streams_of[2], (4, C, C), C ** -0.5, 1.0, (), jnp.float32)
    mix_detail = centred(streams_of[3], (3, C, C), C ** -0.5, 1.0, (), jnp.float32)
    skip_weight = centred(streams_of[4], (C, C), C ** -0.5, 1.0, (), jnp.float32)
    bias_vector = jnp.clip(jax.random.uniform(streams_of[5], (C,), jnp.float32, -0.5, 0.5), -0.5, 0.5)
    return dict(ocean_field=ocean_field, cotangent=cotangent, mix_coarse=mix_coarse, mix_detail=mix_detail, skip_weight=skip_weight, bias_vector=bias_vector)


low_taps = (-0.010597401785069032, 0.0328830116668852, 0.030841381835560764, -0.18703481171909309, -0.027983769416859854, 0.6308807679298589, 0.7148465705529157, 0.2303778133088965)
high_taps = (-0.2303778133088965, 0.7148465705529157, -0.6308807679298589, -0.027983769416859854, 0.18703481171909309, 0.030841381835560764, -0.0328830116668852, -0.010597401785069032)

def wrap_lon(values, extent):
    return jnp.concatenate([values[..., -extent:], values, values[..., :extent]], axis=3)

def zero_lat(values, extent):
    return jnp.pad(values, ((0, 0), (0, 0), (extent, extent), (0, 0)))

def filter_pass(padded, along, length, tap_list):
    summed = tap_list[0] * lax.slice_in_dim(padded, 0, 2 * length - 1, 2, along)
    for offset in range(1, 8):
        summed = summed + tap_list[offset] * lax.slice_in_dim(padded, offset, offset + 2 * length - 1, 2, along)
    return summed

def shifted(padded, offset, length, along):
    return lax.slice_in_dim(padded, offset, offset + length, 1, along)

def upsample_pass(low_padded, high_padded, along, length):

    def halves(padded, tap_list):
        even_part = tap_list[1] * shifted(padded, 3, length, along) + tap_list[3] * shifted(padded, 2, length, along) + tap_list[5] * shifted(padded, 1, length, along) + tap_list[7] * shifted(padded, 0, length, along)
        odd_part = tap_list[0] * shifted(padded, 4, length, along) + tap_list[2] * shifted(padded, 3, length, along) + tap_list[4] * shifted(padded, 2, length, along) + tap_list[6] * shifted(padded, 1, length, along)
        return (even_part, odd_part)
    even_part, odd_part = halves(low_padded, low_taps)
    if high_padded is not None:
        even_high, odd_high = halves(high_padded, high_taps)
        even_part = even_part + even_high
        odd_part = odd_part + odd_high
    merged = jnp.stack([even_part, odd_part], axis=along + 1)
    new_shape = list(even_part.shape)
    new_shape[along] = 2 * length
    return merged.reshape(new_shape)

def analyze(values, details):
    lon_len = values.shape[3] // 2
    lat_len = values.shape[2] // 2
    tap_sets = (low_taps, high_taps) if details else (low_taps,)
    padded = wrap_lon(values, 3)
    lon_parts = jnp.concatenate([filter_pass(padded, 3, lon_len, tap_list) for tap_list in tap_sets], 0)
    padded = zero_lat(lon_parts, 3)
    lat_low = filter_pass(padded, 2, lat_len, low_taps)
    if not details:
        return lat_low
    lat_high = filter_pass(padded, 2, lat_len, high_taps)
    return (lat_low[0:1], jnp.stack([lat_high[0], lat_low[1], lat_high[1]], 0))

def synthesize(approx, detail):
    lat_len = approx.shape[2]
    lon_len = approx.shape[3]
    if detail is None:
        padded = zero_lat(approx, 2)
        rows_up = upsample_pass(padded, None, 2, lat_len)
        padded = wrap_lon(rows_up, 2)
        return upsample_pass(padded, None, 3, lon_len)
    stacked = jnp.concatenate([approx, detail[1:2], detail[0:1], detail[2:3]], 0)
    padded = zero_lat(stacked, 2)
    rows_up = upsample_pass(padded[0:2], padded[2:4], 2, lat_len)
    padded = wrap_lon(rows_up, 2)
    return upsample_pass(padded[0:1], padded[1:2], 3, lon_len)

def mixing(coefficients, weights):
    return jnp.einsum('sirl,sio->sorl', coefficients, weights, precision=lax.Precision.HIGHEST)

def unmixing(coefficients, weights):
    return jnp.einsum('sorl,sio->sirl', coefficients, weights, precision=lax.Precision.HIGHEST)

def contraction(first_coef, second_coef):
    return jnp.einsum('sirl,sorl->sio', first_coef, second_coef, precision=lax.Precision.HIGHEST)

def transform(values):
    level_one = analyze(values, False)
    level_two = analyze(level_one, False)
    approx, detail_three = analyze(level_two, True)
    coarse_low, detail_four = analyze(approx, True)
    return (jnp.concatenate([coarse_low, detail_four], 0), detail_three)

def rebuild(coarse, detail_three):
    level_three = synthesize(coarse[0:1], coarse[1:4])
    level_two = synthesize(level_three, detail_three)
    return synthesize(synthesize(level_two, None), None)[0]

def gelu_slope(pre_act):
    cumulative = 0.5 * (1.0 + jax.scipy.special.erf(pre_act / math.sqrt(2.0)))
    density = jnp.exp(-0.5 * pre_act * pre_act) / math.sqrt(2.0 * math.pi)
    return cumulative + pre_act * density

def reference(ocean_field, cotangent, mix_coarse, mix_detail, skip_weight, bias_vector):
    coarse, detail_three = transform(ocean_field[None])
    kernel = rebuild(mixing(coarse, mix_coarse), mixing(detail_three, mix_detail))
    pre_act = kernel + jnp.einsum('irl,io->orl', ocean_field, skip_weight, precision=lax.Precision.HIGHEST) + bias_vector[:, None, None]
    activated = jax.nn.gelu(pre_act, approximate=False).astype(jnp.bfloat16)
    grad_pre = cotangent.astype(jnp.float32) * gelu_slope(pre_act)
    grad_coarse, grad_detail = transform(grad_pre[None])
    cell_count = NLAT * NLON
    grad_mix_coarse = contraction(coarse, grad_coarse) / math.sqrt(cell_count // 256)
    grad_mix_detail = contraction(detail_three, grad_detail) / math.sqrt(cell_count // 64)
    grad_skip = jnp.einsum('irl,orl->io', ocean_field, grad_pre, precision=lax.Precision.HIGHEST) / math.sqrt(cell_count)
    grad_bias = lax.optimization_barrier(jnp.sum(grad_pre, axis=(1, 2))) / math.sqrt(cell_count)
    grad_field = rebuild(unmixing(grad_coarse, mix_coarse), unmixing(grad_detail, mix_detail))
    grad_field = grad_field + jnp.einsum('orl,io->irl', grad_pre, skip_weight, precision=lax.Precision.HIGHEST)
    return (activated, grad_field, grad_mix_coarse, grad_mix_detail, grad_skip, grad_bias)
```

```python
import math

import jax
import jax.numpy as jnp
import numpy as np
from jax import lax
from jax.experimental import pallas as pl
from jax.experimental.pallas import tpu as pltpu
from jax.sharding import PartitionSpec as P
from ml_dtypes import bfloat16

F32 = jnp.float32
BF16 = jnp.bfloat16

low_taps = (
    -0.010597401785069032,
    0.0328830116668852,
    0.030841381835560764,
    -0.18703481171909309,
    -0.027983769416859854,
    0.6308807679298589,
    0.7148465705529157,
    0.2303778133088965,
)
high_taps = (
    -0.2303778133088965,
    0.7148465705529157,
    -0.6308807679298589,
    -0.027983769416859854,
    0.18703481171909309,
    0.030841381835560764,
    -0.0328830116668852,
    -0.010597401785069032,
)

CHANNELS = 32
LAT_PARTS = 4
LAT_BLOCK = 64
LON_BLOCK = 128
LAT_BAND = (0, 1, 0, 1, 3, 2, 3)
LON_BAND = (0, 0, 1, 1, 2, 3, 3)
LO_LANES = 42
HI_LANE = 64


def level_matrix(size, taps, periodic):
    matrix = np.zeros((size // 2, size))
    for k in range(size // 2):
        for j in range(8):
            m = 2 * k + j - 3
            if periodic:
                matrix[k, m % size] += taps[j]
            elif 0 <= m < size:
                matrix[k, m] += taps[j]
    return matrix


def composed(size, periodic):
    two = level_matrix(size // 2, low_taps, periodic) @ level_matrix(size, low_taps, periodic)
    three_low = level_matrix(size // 4, low_taps, periodic) @ two
    three_high = level_matrix(size // 4, high_taps, periodic) @ two
    four_low = level_matrix(size // 8, low_taps, periodic) @ three_low
    four_high = level_matrix(size // 8, high_taps, periodic) @ three_low
    return (four_low, four_high, three_low, three_high)


def lane_table():
    lanes = [None] * 128
    inner = []
    for s in range(7):
        count = 14 if s < 4 else 22
        for e in range(6):
            lanes[s * 6 + e] = (s, e)
            lanes[HI_LANE + s * 6 + e] = (s, count - 6 + e)
        inner += [(s, e) for e in range(6, count - 6)]
    free = [lane for lane in range(128) if lanes[lane] is None]
    for lane, entry in zip(free, inner):
        lanes[lane] = entry
    return lanes


LANES = lane_table()
SUBBAND_OF_LANE = np.array([-1 if entry is None else entry[0] for entry in LANES])


def lon_weights():
    maps = composed(8 * LON_BLOCK, True)
    start = 3 * LON_BLOCK
    weights = np.zeros((4, LON_BLOCK, 128))
    for lane, entry in enumerate(LANES):
        if entry is None:
            continue
        s, e = entry
        per_block = 8 if s < 4 else 16
        row = maps[LON_BAND[s]][3 * per_block - 3 + e]
        weights[LAT_BAND[s], :, lane] = row[start : start + LON_BLOCK]
    return weights.reshape(4 * LON_BLOCK, 128)


def row_entries(part):
    top4, bottom4 = list(range(6)) + [None] * 2, list(range(4, 10)) + [None] * 2
    top3, bottom3 = list(range(8)), list(range(8, 14)) + [None] * 2
    four = bottom4 + top4 if part % 2 == 0 else top4 + bottom4
    three = bottom3 + top3 if part % 2 == 0 else top3 + bottom3
    four[14:16] = [8, 9] if part < 2 else [0, 1]
    return four, three


def lat_weights():
    maps = composed(LAT_PARTS * LAT_BLOCK, False)
    weights = np.zeros((LAT_PARTS, 4, 16, LAT_BLOCK))
    for part in range(LAT_PARTS):
        entries = row_entries(part)
        for band in range(4):
            per_block = 4 if band < 2 else 8
            for row, e in enumerate(entries[0 if band < 2 else 1]):
                k = per_block * part - 3 + e if e is not None else -1
                if 0 <= k < per_block * LAT_PARTS:
                    weights[part, band, row] = maps[band][
                        k, part * LAT_BLOCK : (part + 1) * LAT_BLOCK
                    ]
    return weights.reshape(LAT_PARTS, 64, LAT_BLOCK)


def own_mask():
    mask = np.ones((LAT_PARTS, 16, 128), np.float32)
    four = (SUBBAND_OF_LANE >= 0) & (SUBBAND_OF_LANE < 4)
    for part in range(LAT_PARTS):
        bottom = 0 if part % 2 == 0 else 8
        for row in (bottom, bottom + 1, 14, 15):
            mask[part, row, four] = 0.0
    return mask


def high_low(matrix):
    matrix = matrix.astype(np.float32)
    high = matrix.astype(bfloat16)
    low = (matrix - high.astype(np.float32)).astype(bfloat16)
    return np.stack([high, low], axis=-3)


LON = lon_weights()
LAT = lat_weights()
LON_A = high_low(LON)
LON_S = high_low(LON.T)
LAT_A = high_low(np.stack([np.kron(np.eye(4), LAT[p]) for p in range(LAT_PARTS)]))
LAT_S = high_low(np.stack([np.kron(np.eye(4), LAT[p].T) for p in range(LAT_PARTS)]))
OWN = own_mask()


def split(x):
    high = x.astype(BF16)
    low = (x - high.astype(F32)).astype(BF16)
    return high, low


def dot(a, b):
    return jnp.dot(a, b, preferred_element_type=F32)


def dot_nt(a, b):
    return lax.dot_general(a, b, (((1,), (1,)), ((), ())), preferred_element_type=F32)


def dot3(a, b, product=dot):
    return product(a[0], b[0]) + (product(a[0], b[1]) + product(a[1], b[0]))


def both(ref):
    return ref[0], ref[1]


def grouped(x):
    return jnp.concatenate([x[4 * g : 4 * g + 4].reshape(256, 128) for g in range(8)], axis=1)


def tiled(x):
    return jnp.concatenate(
        [x[:, 8 * t : 8 * t + 8, :].reshape(256, 128) for t in range(8)], axis=1
    )


def analysis(groups, lat, lon):
    rows = dot3(lat, split(groups))
    blocks = []
    for g in range(8):
        part = rows[:, 128 * g : 128 * g + 128].reshape(4, 4, 16, 128)
        blocks.append(
            jnp.concatenate([part[:, b].reshape(64, 128) for b in range(4)], axis=1)
        )
    return dot3(split(jnp.concatenate(blocks, axis=0)), lon).reshape(32, 16, 128)


def synthesis(frame, lat, lon):
    wide = dot3(split(frame), lon).reshape(8, 4, 16, 512)
    groups = []
    for g in range(8):
        part = jnp.stack(
            [wide[g, :, :, 128 * b : 128 * b + 128] for b in range(4)], axis=1
        )
        groups.append(part.reshape(256, 128))
    return dot3(lat, split(jnp.concatenate(groups, axis=1)))


def lane_index(shape):
    return lax.broadcasted_iota(jnp.int32, shape, len(shape) - 1)


def subband_lanes(shape, s):
    lane = lax.rem(lane_index(shape), 128)
    mask = (lane >= 6 * s) & (lane < 6 * s + 6)
    mask = mask | ((lane >= HI_LANE + 6 * s) & (lane < HI_LANE + 6 * s + 6))
    inner = [i for i in range(128) if LANES[i] is not None and LANES[i][0] == s]
    inner = [i for i in inner if not (i < LO_LANES or HI_LANE <= i < HI_LANE + LO_LANES)]
    runs = []
    for i in inner:
        if runs and runs[-1][1] == i:
            runs[-1][1] = i + 1
        else:
            runs.append([i, i + 1])
    for first, last in runs:
        mask = mask | ((lane >= first) & (lane < last))
    return mask


def roll64(x):
    return pltpu.roll(x, 64, 2)


def whole(frame_a, frame_b, from_left, from_right):
    lane = lane_index(frame_a.shape)
    low = lane < LO_LANES
    high = (lane >= HI_LANE) & (lane < HI_LANE + LO_LANES)
    frame_a = frame_a + jnp.where(low, from_left, 0.0) + jnp.where(high, roll64(from_right), 0.0)
    frame_b = frame_b + jnp.where(low, roll64(from_left), 0.0) + jnp.where(high, from_right, 0.0)
    return frame_a, frame_b


def mixed(frame_a, frame_b, weights_ref):
    data = split(
        jnp.concatenate([frame_a.reshape(256, 128), frame_b.reshape(256, 128)], axis=1)
    )
    result = jnp.zeros((256, 256), F32)
    for s in range(7):
        product = dot3((weights_ref[s, 0], weights_ref[s, 1]), data)
        result = jnp.where(subband_lanes((256, 256), s), product, result)
    return jnp.concatenate(
        [result[:, :128].reshape(32, 8, 128), result[:, 128:].reshape(32, 8, 128)], axis=1
    ).reshape(512, 128)


def store_frame(frame, a_ref, b_ref, far_ref):
    a_ref[...] = frame[:, :8]
    b_ref[...] = frame[:, 8:]
    far_ref[...] = frame[:, 14:16]


def analysis_kernel(part_ref, x_ref, lat_ref, lon_ref, a_ref, b_ref, far_ref):
    frame = analysis(grouped(x_ref[...]), both(lat_ref[0]), both(lon_ref))
    store_frame(frame, a_ref, b_ref, far_ref)


def expand_matrix():
    row = lax.broadcasted_iota(jnp.int32, (256, 32), 0)
    return (row // 8 == lane_index((256, 32))).astype(BF16)


def same_row(shape):
    row = lax.broadcasted_iota(jnp.int32, shape, 0)
    return lax.rem(row, 8) == lax.rem(lane_index(shape), 8)


def prepare_kernel(x_ref, coarse_ref, detail_ref, skip_ref, bias_ref, mix_ref, unmix_ref, pre_ref):
    expand = expand_matrix()
    diagonal = same_row((256, 256))
    for s in range(8):
        weight = coarse_ref[s] if s < 4 else (detail_ref[s - 4] if s < 7 else skip_ref[...])
        for k, part in enumerate(split(weight)):
            forward = dot_nt(dot_nt(expand, part).astype(BF16), expand)
            backward = dot_nt(dot(expand, part).astype(BF16), expand)
            mix_ref[s, k] = jnp.where(diagonal, forward, 0.0).astype(BF16)
            unmix_ref[s, k] = jnp.where(diagonal, backward, 0.0).astype(BF16)
    product = dot3((mix_ref[7, 0], mix_ref[7, 1]), split(tiled(x_ref[...])))
    bias = bias_ref[...]
    for t in range(8):
        pre_ref[:, 8 * t : 8 * t + 8, :] = (
            product[:, 128 * t : 128 * t + 128].reshape(32, 8, 128) + bias
        )


def lat_sum_kernel(
    part_ref, mask_ref, a_ref, b_ref, near_ref, other_ref, far_ref, fa_ref, fb_ref, low_ref, high_ref
):
    shape = (32, 8, 128)
    keep = lax.broadcasted_iota(jnp.int32, shape, 1) < 6
    mask = mask_ref[0]
    frame_a = a_ref[...] * mask[None, :8] + jnp.where(keep, near_ref[...], 0.0)
    frame_b = b_ref[...] * mask[None, 8:] + jnp.where(keep, other_ref[...], 0.0)
    fa_ref[...] = frame_a
    fb_ref[...] = frame_b
    lane = lane_index((32, 2, 128))
    four = lane < 0
    for s in range(4):
        four = four | subband_lanes((32, 2, 128), s)
    fb_ref[:, 6:8, :] += jnp.where(four, far_ref[...], 0.0)
    frame_b = fb_ref[...]
    first = lane_index(shape) < 64
    low_ref[...] = jnp.where(first, frame_a, roll64(frame_b))
    high_ref[...] = jnp.where(first, roll64(frame_a), frame_b)


def forward_kernel(
    part_ref,
    fa_ref,
    fb_ref,
    left_ref,
    right_ref,
    pre_ref,
    cot_ref,
    mix_ref,
    lat_a_ref,
    lat_s_ref,
    lon_a_ref,
    lon_s_ref,
    act_ref,
    grad_ref,
    ca_ref,
    cb_ref,
    a_ref,
    b_ref,
    far_ref,
):
    frame_a, frame_b = whole(fa_ref[...], fb_ref[...], left_ref[...], right_ref[...])
    ca_ref[...] = frame_a
    cb_ref[...] = frame_b
    kernel = synthesis(mixed(frame_a, frame_b, mix_ref), both(lat_s_ref[0]), both(lon_s_ref))
    grads = []
    for g in range(8):
        channels = slice(4 * g, 4 * g + 4)
        pre = kernel[:, 128 * g : 128 * g + 128] + pre_ref[channels].reshape(256, 128)
        cumulative = 0.5 * (1.0 + lax.erf(pre * math.sqrt(0.5)))
        density = jnp.exp(-0.5 * pre * pre) * (1.0 / math.sqrt(2.0 * math.pi))
        act_ref[channels] = (pre * cumulative).astype(BF16).reshape(4, 64, 128)
        grad = cot_ref[channels].astype(F32).reshape(256, 128) * (cumulative + pre * density)
        grad_ref[channels] = grad.reshape(4, 64, 128)
        grads.append(grad)
    frame = analysis(jnp.concatenate(grads, axis=1), both(lat_a_ref[0]), both(lon_a_ref))
    store_frame(frame, a_ref, b_ref, far_ref)


def weights_kernel(x_ref, g_ref, ca_ref, cb_ref, a_ref, b_ref, sum_ref):
    diagonal = same_row((256, 256))

    def reduced(product):
        rows = jnp.where(diagonal, product, 0.0).reshape(32, 8, 256)
        return split(jnp.sum(rows, axis=1))

    def placed(parts, offset):
        row = lax.broadcasted_iota(jnp.int32, (256, 128), 0)
        place = (row // 8 + offset == lane_index((256, 128))).astype(BF16)
        return dot(parts[0], place) + dot(parts[1], place)

    coef = jnp.concatenate([ca_ref[...].reshape(256, 128), cb_ref[...].reshape(256, 128)], axis=1)
    grad = split(
        jnp.concatenate([a_ref[...].reshape(256, 128), b_ref[...].reshape(256, 128)], axis=1)
    )
    sums = [jnp.zeros((32, 128), F32), jnp.zeros((32, 128), F32)]
    for s in range(7):
        chosen = split(jnp.where(subband_lanes((256, 256), s), coef, 0.0))
        product = dot3(chosen, grad, dot_nt)
        sums[s // 4] = sums[s // 4] + placed(reduced(product), 32 * (s % 4))
    field = split(tiled(x_ref[...]))
    grad_pre = split(tiled(g_ref[...]))
    sums[1] = sums[1] + placed(reduced(dot3(field, grad_pre, dot_nt)), 96)
    ones = jnp.ones((8, 1024), BF16)
    bias = split(dot_nt(ones, grad_pre[0]) + dot_nt(ones, grad_pre[1]))
    sum_ref[0:32] = sums[0]
    sum_ref[32:64] = sums[1]
    sum_ref[64:72] = placed(bias, 0)


def skip_back_kernel(g_ref, unmix_ref, out_ref):
    product = dot3((unmix_ref[7, 0], unmix_ref[7, 1]), split(tiled(g_ref[...])))
    for t in range(8):
        out_ref[:, 8 * t : 8 * t + 8, :] = product[:, 128 * t : 128 * t + 128].reshape(32, 8, 128)


def backward_kernel(
    part_ref, fa_ref, fb_ref, left_ref, right_ref, skip_ref, unmix_ref, lat_s_ref, lon_s_ref, out_ref
):
    frame_a, frame_b = whole(fa_ref[...], fb_ref[...], left_ref[...], right_ref[...])
    field = synthesis(mixed(frame_a, frame_b, unmix_ref), both(lat_s_ref[0]), both(lon_s_ref))
    for g in range(8):
        channels = slice(4 * g, 4 * g + 4)
        out_ref[channels] = skip_ref[channels] + field[:, 128 * g : 128 * g + 128].reshape(
            4, 64, 128
        )


def full_spec(shape):
    return pl.BlockSpec(shape, lambda *_: (0,) * len(shape))


def part_spec(shape):
    return pl.BlockSpec(shape, lambda _, part: (part[0],) + (0,) * (len(shape) - 1))


def shape_of(*shape, dtype=F32):
    return jax.ShapeDtypeStruct(shape, dtype)


def call(kernel, outs, args, part=None, by_part=()):
    in_specs = [
        part_spec((1,) + arg.shape[1:]) if i in by_part else full_spec(arg.shape)
        for i, arg in enumerate(args)
    ]
    out_specs = [full_spec(out.shape) for out in outs]
    params = pltpu.CompilerParams(vmem_limit_bytes=48 * 1024 * 1024)
    if part is None:
        return pl.pallas_call(
            kernel,
            grid=(1,),
            in_specs=in_specs,
            out_specs=out_specs,
            out_shape=list(outs),
            compiler_params=params,
        )(*args)
    grid_spec = pltpu.PrefetchScalarGridSpec(
        num_scalar_prefetch=1, grid=(1,), in_specs=in_specs, out_specs=out_specs
    )
    return pl.pallas_call(
        kernel, grid_spec=grid_spec, out_shape=list(outs), compiler_params=params
    )(part, *args)


TILE = shape_of(32, 8, 128)
FAR = shape_of(32, 2, 128)
FIELD = shape_of(32, 64, 128)


def exchange(a, b, far, part):
    near = lax.ppermute(a, "lat", [(i, i ^ 1) for i in range(LAT_PARTS)])
    other = lax.ppermute(b, "lat", [(1, 2), (2, 1)])
    far = lax.ppermute(far, "lat", [(i, i ^ 2) for i in range(LAT_PARTS)])
    fa, fb, low, high = call(
        lat_sum_kernel, (TILE,) * 4, (jnp.asarray(OWN), a, b, near, other, far), part, (0,)
    )
    count = lax.axis_size("lon")
    from_left = lax.ppermute(high, "lon", [(i, (i + 1) % count) for i in range(count)])
    from_right = lax.ppermute(low, "lon", [((i + 1) % count, i) for i in range(count)])
    return fa, fb, from_left, from_right


def total(values):
    for step in (1, 2):
        values = values + lax.ppermute(
            values, "lat", [(i, i ^ step) for i in range(lax.axis_size("lat"))]
        )
    for step in (1, 2, 4, 8, 16, 32):
        values = values + lax.ppermute(
            values, "lon", [(i, i ^ step) for i in range(lax.axis_size("lon"))]
        )
    return values


def on_device(ocean_field, cotangent, mix_coarse, mix_detail, skip_weight, bias_vector):
    part = lax.axis_index("lat").astype(jnp.int32).reshape(1)
    lat_a, lat_s = jnp.asarray(LAT_A), jnp.asarray(LAT_S)
    lon_a, lon_s = jnp.asarray(LON_A), jnp.asarray(LON_S)
    a, b, far = call(
        analysis_kernel, (TILE, TILE, FAR), (ocean_field, lat_a, lon_a), part, (1,)
    )
    weights = shape_of(8, 2, 256, 256, dtype=BF16)
    bias = jnp.broadcast_to(bias_vector[:, None, None], (CHANNELS, 1, 128))
    mix, unmix, pre = call(
        prepare_kernel,
        (weights, weights, FIELD),
        (ocean_field, mix_coarse, mix_detail, skip_weight, bias),
    )
    fa, fb, from_left, from_right = exchange(a, b, far, part)
    activated, grad_pre, coef_a, coef_b, a, b, far = call(
        forward_kernel,
        (shape_of(32, 64, 128, dtype=BF16), FIELD, TILE, TILE, TILE, TILE, FAR),
        (fa, fb, from_left, from_right, pre, cotangent, mix, lat_a, lat_s, lon_a, lon_s),
        part,
        (7, 8),
    )
    (sums,) = call(
        weights_kernel, (shape_of(72, 128),), (ocean_field, grad_pre, coef_a, coef_b, a, b)
    )
    (skip_back,) = call(skip_back_kernel, (FIELD,), (grad_pre, unmix))
    fa, fb, from_left, from_right = exchange(a, b, far, part)
    (grad_field,) = call(
        backward_kernel,
        (FIELD,),
        (fa, fb, from_left, from_right, skip_back, unmix, lat_s, lon_s),
        part,
        (6,),
    )
    sums = total(sums)
    cells = LAT_PARTS * LAT_BLOCK * LON_BLOCK * lax.axis_size("lon")
    coarse = sums[0:32].reshape(32, 4, 32).transpose(1, 0, 2) / math.sqrt(cells // 256)
    detail = sums[32:64, :96].reshape(32, 3, 32).transpose(1, 0, 2) / math.sqrt(cells // 64)
    grad_skip = sums[32:64, 96:] / math.sqrt(cells)
    grad_bias = sums[64, :32] / math.sqrt(cells)
    return (activated, grad_field, coarse, detail, grad_skip, grad_bias)


def solution(mesh):
    return jax.shard_map(
        on_device,
        mesh=mesh,
        in_specs=(P(None, "lat", "lon"), P(None, "lat", "lon"), P(), P(), P(), P()),
        out_specs=(P(None, "lat", "lon"), P(None, "lat", "lon"), P(), P(), P(), P()),
        check_vma=False,
    )
```

```python
import functools
import math

import jax
import jax.numpy as jnp
import numpy as np
from jax import lax
from jax.experimental import pallas as pl
from jax.experimental.pallas import tpu as pltpu
from jax.sharding import PartitionSpec as P
from ml_dtypes import bfloat16

F32 = jnp.float32
BF16 = jnp.bfloat16

low_taps = (
    -0.010597401785069032,
    0.0328830116668852,
    0.030841381835560764,
    -0.18703481171909309,
    -0.027983769416859854,
    0.6308807679298589,
    0.7148465705529157,
    0.2303778133088965,
)
high_taps = (
    -0.2303778133088965,
    0.7148465705529157,
    -0.6308807679298589,
    -0.027983769416859854,
    0.18703481171909309,
    0.030841381835560764,
    -0.0328830116668852,
    -0.010597401785069032,
)

CHANNELS = 32
LAT_PARTS = 4
LAT_BLOCK = 64
LON_BLOCK = 128
LAT_BAND = (0, 1, 0, 1, 3, 2, 3)
LON_BAND = (0, 0, 1, 1, 2, 3, 3)
LO_LANES = 42
HI_LANE = 64


def level_matrix(size, taps, periodic):
    matrix = np.zeros((size // 2, size))
    for k in range(size // 2):
        for j in range(8):
            m = 2 * k + j - 3
            if periodic:
                matrix[k, m % size] += taps[j]
            elif 0 <= m < size:
                matrix[k, m] += taps[j]
    return matrix


def composed(size, periodic):
    two = level_matrix(size // 2, low_taps, periodic) @ level_matrix(size, low_taps, periodic)
    three_low = level_matrix(size // 4, low_taps, periodic) @ two
    three_high = level_matrix(size // 4, high_taps, periodic) @ two
    four_low = level_matrix(size // 8, low_taps, periodic) @ three_low
    four_high = level_matrix(size // 8, high_taps, periodic) @ three_low
    return (four_low, four_high, three_low, three_high)


def lane_table():
    lanes = [None] * 128
    inner = []
    for s in range(7):
        count = 14 if s < 4 else 22
        for e in range(6):
            lanes[s * 6 + e] = (s, e)
            lanes[HI_LANE + s * 6 + e] = (s, count - 6 + e)
        inner += [(s, e) for e in range(6, count - 6)]
    free = [lane for lane in range(128) if lanes[lane] is None]
    for lane, entry in zip(free, inner):
        lanes[lane] = entry
    return lanes


LANES = lane_table()
SUBBAND_OF_LANE = np.array([-1 if entry is None else entry[0] for entry in LANES])


def lon_weights():
    maps = composed(8 * LON_BLOCK, True)
    start = 3 * LON_BLOCK
    weights = np.zeros((4, LON_BLOCK, 128))
    for lane, entry in enumerate(LANES):
        if entry is None:
            continue
        s, e = entry
        per_block = 8 if s < 4 else 16
        row = maps[LON_BAND[s]][3 * per_block - 3 + e]
        weights[LAT_BAND[s], :, lane] = row[start : start + LON_BLOCK]
    return weights.reshape(4 * LON_BLOCK, 128)


def row_entries(part):
    top4, bottom4 = list(range(6)) + [None] * 2, list(range(4, 10)) + [None] * 2
    top3, bottom3 = list(range(8)), list(range(8, 14)) + [None] * 2
    four = bottom4 + top4 if part % 2 == 0 else top4 + bottom4
    three = bottom3 + top3 if part % 2 == 0 else top3 + bottom3
    four[14:16] = [8, 9] if part < 2 else [0, 1]
    return four, three


def lat_weights():
    maps = composed(LAT_PARTS * LAT_BLOCK, False)
    weights = np.zeros((LAT_PARTS, 4, 16, LAT_BLOCK))
    for part in range(LAT_PARTS):
        entries = row_entries(part)
        for band in range(4):
            per_block = 4 if band < 2 else 8
            for row, e in enumerate(entries[0 if band < 2 else 1]):
                k = per_block * part - 3 + e if e is not None else -1
                if 0 <= k < per_block * LAT_PARTS:
                    weights[part, band, row] = maps[band][
                        k, part * LAT_BLOCK : (part + 1) * LAT_BLOCK
                    ]
    return weights.reshape(LAT_PARTS, 64, LAT_BLOCK)


def own_mask():
    mask = np.ones((LAT_PARTS, 16, 128), np.float32)
    four = (SUBBAND_OF_LANE >= 0) & (SUBBAND_OF_LANE < 4)
    for part in range(LAT_PARTS):
        bottom = 0 if part % 2 == 0 else 8
        for row in (bottom, bottom + 1, 14, 15):
            mask[part, row, four] = 0.0
    return mask


def high_low(matrix):
    matrix = matrix.astype(np.float32)
    high = matrix.astype(bfloat16)
    low = (matrix - high.astype(np.float32)).astype(bfloat16)
    return np.stack([high, low], axis=-3)


LON = lon_weights()
LAT = lat_weights()
LON_A = high_low(LON)
LON_S = high_low(LON.T)
LAT_A = high_low(np.stack([np.tile(LAT[p], (1, 4)) for p in range(LAT_PARTS)]))
LAT_S = high_low(np.stack([np.tile(LAT[p].T, (1, 4)) for p in range(LAT_PARTS)]))
OWN = own_mask()
SUBBANDS = np.tile(SUBBAND_OF_LANE.astype(np.float32), (8, 1))


def split(x):
    high = x.astype(BF16)
    low = (x - high.astype(F32)).astype(BF16)
    return high, low


def dot(a, b):
    return jnp.dot(a, b, preferred_element_type=F32)


def dot_nt(a, b):
    return lax.dot_general(a, b, (((1,), (1,)), ((), ())), preferred_element_type=F32)


def dot3(a, b, product=dot):
    return product(a[0], b[0]) + (product(a[0], b[1]) + product(a[1], b[0]))


def both(ref):
    return ref[0], ref[1]


def block_diagonal(ref):
    row = lax.broadcasted_iota(jnp.int32, (256, 256), 0)
    keep = row // 64 == lane_index((256, 256)) // 64
    return tuple(
        jnp.where(keep, jnp.concatenate([ref[0, k]] * 4, axis=0), 0.0).astype(BF16)
        for k in range(2)
    )


def grouped(x):
    return jnp.concatenate([x[4 * g : 4 * g + 4].reshape(256, 128) for g in range(8)], axis=1)


def tiled(x):
    return jnp.concatenate(
        [x[:, 8 * t : 8 * t + 8, :].reshape(256, 128) for t in range(8)], axis=1
    )


def analysis(groups, lat, lon):
    rows = dot3(lat, split(groups))
    blocks = []
    for g in range(8):
        part = rows[:, 128 * g : 128 * g + 128].reshape(4, 4, 16, 128)
        blocks.append(
            jnp.concatenate([part[:, b].reshape(64, 128) for b in range(4)], axis=1)
        )
    return dot3(split(jnp.concatenate(blocks, axis=0)), lon).reshape(32, 16, 128)


def synthesis(frame, lat, lon):
    wide = dot3(split(frame), lon).reshape(8, 4, 16, 512)
    groups = []
    for g in range(8):
        part = jnp.stack(
            [wide[g, :, :, 128 * b : 128 * b + 128] for b in range(4)], axis=1
        )
        groups.append(part.reshape(256, 128))
    return dot3(lat, split(jnp.concatenate(groups, axis=1)))


def lane_index(shape):
    return lax.broadcasted_iota(jnp.int32, shape, len(shape) - 1)


def roll64(x):
    return pltpu.roll(x, 64, 2)


def whole(frame_a, frame_b, from_left, from_right):
    lane = lane_index(frame_a.shape)
    low = lane < LO_LANES
    high = (lane >= HI_LANE) & (lane < HI_LANE + LO_LANES)
    frame_a = frame_a + jnp.where(low, from_left, 0.0) + jnp.where(high, roll64(from_right), 0.0)
    frame_b = frame_b + jnp.where(low, roll64(from_left), 0.0) + jnp.where(high, from_right, 0.0)
    return frame_a, frame_b


def by_row(frame_a, frame_b, scratch):
    scratch[...] = jnp.concatenate([frame_a, frame_b], axis=1).reshape(512, 128)
    return jnp.concatenate([scratch[pl.ds(r, 32, stride=16), :] for r in range(16)], axis=1)


def stacked(data, subbands):
    lanes = jnp.concatenate([subbands[0:1]] * 16, axis=1)
    return [
        jnp.concatenate(
            [jnp.where(lanes == float(s), part, 0.0).astype(BF16) for s in range(7)], axis=0
        )
        for part in (data, data - data.astype(BF16).astype(F32))
    ]


def mixed(frame_a, frame_b, weights, subbands, scratch):
    data = stacked(by_row(frame_a, frame_b, scratch), subbands)
    high, low = split(weights)
    double = dot(jnp.concatenate([high, low], axis=0), data[0])
    result = double[:32] + (double[32:] + dot(high, data[1]))
    for r in range(16):
        scratch[pl.ds(r, 32, stride=16), :] = result[:, 128 * r : 128 * r + 128]
    return scratch[...]


def store_frame(frame, a_ref, b_ref, far_ref):
    a_ref[...] = frame[:, :8]
    b_ref[...] = frame[:, 8:]
    far_ref[...] = frame[:, 14:16]


def analysis_kernel(part_ref, x_ref, lat_ref, lon_ref, a_ref, b_ref, far_ref):
    frame = analysis(grouped(x_ref[...]), block_diagonal(lat_ref), both(lon_ref))
    store_frame(frame, a_ref, b_ref, far_ref)


def expand_matrix():
    row = lax.broadcasted_iota(jnp.int32, (256, 32), 0)
    return (row // 8 == lane_index((256, 32))).astype(BF16)


def same_row(shape):
    row = lax.broadcasted_iota(jnp.int32, shape, 0)
    return lax.rem(row, 8) == lax.rem(lane_index(shape), 8)


def expanded(weight, product):
    expand = expand_matrix()
    diagonal = same_row((256, 256))
    return tuple(
        jnp.where(diagonal, dot_nt(product(expand, part).astype(BF16), expand), 0.0).astype(BF16)
        for part in split(weight)
    )


def skip_kernel(x_ref, skip_ref, bias_ref, pre_ref):
    weight = expanded(skip_ref[...], dot_nt)
    product = dot3(weight, split(tiled(x_ref[...])))
    bias = jnp.sum(expand_matrix().astype(F32) * bias_ref[...], axis=1, keepdims=True)
    for t in range(8):
        pre_ref[:, 8 * t : 8 * t + 8, :] = (
            product[:, 128 * t : 128 * t + 128] + bias
        ).reshape(32, 8, 128)


def lat_sum_kernel(
    part_ref,
    mask_ref,
    a_ref,
    b_ref,
    near_ref,
    other_ref,
    far_ref,
    subband_ref,
    fa_ref,
    fb_ref,
    low_ref,
    high_ref,
):
    shape = (32, 8, 128)
    keep = lax.broadcasted_iota(jnp.int32, shape, 1) < 6
    mask = mask_ref[0]
    frame_a = a_ref[...] * mask[None, :8] + jnp.where(keep, near_ref[...], 0.0)
    frame_b = b_ref[...] * mask[None, 8:] + jnp.where(keep, other_ref[...], 0.0)
    fa_ref[...] = frame_a
    fb_ref[...] = frame_b
    subband = subband_ref[0:2][None]
    four = (subband >= 0.0) & (subband < 4.0)
    fb_ref[:, 6:8, :] += jnp.where(four, far_ref[...], 0.0)
    frame_b = fb_ref[...]
    first = lane_index(shape) < 64
    low_ref[...] = jnp.where(first, frame_a, roll64(frame_b))
    high_ref[...] = jnp.where(first, roll64(frame_a), frame_b)


def forward_kernel(
    part_ref,
    fa_ref,
    fb_ref,
    left_ref,
    right_ref,
    pre_ref,
    cot_ref,
    coarse_ref,
    detail_ref,
    subband_ref,
    lat_a_ref,
    lat_s_ref,
    lon_a_ref,
    lon_s_ref,
    act_ref,
    grad_ref,
    ca_ref,
    cb_ref,
    a_ref,
    b_ref,
    far_ref,
    scratch,
):
    frame_a, frame_b = whole(fa_ref[...], fb_ref[...], left_ref[...], right_ref[...])
    ca_ref[...] = frame_a
    cb_ref[...] = frame_b
    weights = jnp.concatenate(
        [coarse_ref[s].T for s in range(4)] + [detail_ref[s].T for s in range(3)], axis=1
    )
    frame = mixed(frame_a, frame_b, weights, subband_ref[...], scratch)
    kernel = synthesis(frame, block_diagonal(lat_s_ref), both(lon_s_ref))
    grads = []
    for g in range(8):
        channels = slice(4 * g, 4 * g + 4)
        pre = kernel[:, 128 * g : 128 * g + 128] + pre_ref[channels].reshape(256, 128)
        cumulative = 0.5 * (1.0 + lax.erf(pre * math.sqrt(0.5)))
        density = jnp.exp(-0.5 * pre * pre) * (1.0 / math.sqrt(2.0 * math.pi))
        act_ref[channels] = (pre * cumulative).astype(BF16).reshape(4, 64, 128)
        grad = cot_ref[channels].astype(F32).reshape(256, 128) * (cumulative + pre * density)
        grad_ref[channels] = grad.reshape(4, 64, 128)
        grads.append(grad)
    frame = analysis(jnp.concatenate(grads, axis=1), block_diagonal(lat_a_ref), both(lon_a_ref))
    store_frame(frame, a_ref, b_ref, far_ref)


def weights_kernel(
    x_ref, g_ref, ca_ref, cb_ref, a_ref, b_ref, subband_ref, sum_ref, scratch_c, scratch_g
):
    def placed(parts, offset):
        row = lax.broadcasted_iota(jnp.int32, (256, 128), 0)
        place = (row // 8 + offset == lane_index((256, 128))).astype(BF16)
        return dot(parts[0], place) + dot(parts[1], place)

    coef = stacked(by_row(ca_ref[...], cb_ref[...], scratch_c), subband_ref[...])
    high, low = split(by_row(a_ref[...], b_ref[...], scratch_g))
    double = dot_nt(jnp.concatenate([high, low], axis=0), coef[0])
    mix = double[:32] + (double[32:] + dot_nt(high, coef[1]))
    mix = jnp.concatenate([mix, jnp.zeros((32, 32), F32)], axis=1)
    field = split(tiled(x_ref[...]))
    grad_pre = split(tiled(g_ref[...]))
    product = jnp.where(same_row((256, 256)), dot3(grad_pre, field, dot_nt), 0.0)
    skip = split(jnp.sum(product.reshape(32, 8, 256), axis=1))
    ones = jnp.ones((8, 1024), BF16)
    bias = split(dot_nt(ones, grad_pre[0]) + dot_nt(ones, grad_pre[1]))
    sum_ref[0:32] = mix[:, :128]
    sum_ref[32:64] = mix[:, 128:] + placed(skip, 96)
    sum_ref[64:72] = placed(bias, 0)


def result_kernel(sum_ref, coarse_ref, detail_ref, skip_ref, bias_ref, cells):
    first = sum_ref[0:32].T
    second = sum_ref[32:64].T
    for s in range(4):
        coarse_ref[s] = first[32 * s : 32 * s + 32] * (1.0 / math.sqrt(cells // 256))
    for s in range(3):
        detail_ref[s] = second[32 * s : 32 * s + 32] * (1.0 / math.sqrt(cells // 64))
    skip_ref[...] = second[96:] * (1.0 / math.sqrt(cells))
    bias_ref[...] = sum_ref[64:65, :32] * (1.0 / math.sqrt(cells))


def skip_back_kernel(g_ref, skip_ref, out_ref):
    product = dot3(expanded(skip_ref[...], dot), split(tiled(g_ref[...])))
    for t in range(8):
        out_ref[:, 8 * t : 8 * t + 8, :] = product[:, 128 * t : 128 * t + 128].reshape(32, 8, 128)


def backward_kernel(
    part_ref,
    fa_ref,
    fb_ref,
    left_ref,
    right_ref,
    skip_ref,
    coarse_ref,
    detail_ref,
    subband_ref,
    lat_s_ref,
    lon_s_ref,
    out_ref,
    scratch,
):
    frame_a, frame_b = whole(fa_ref[...], fb_ref[...], left_ref[...], right_ref[...])
    weights = jnp.concatenate(
        [coarse_ref[s] for s in range(4)] + [detail_ref[s] for s in range(3)], axis=1
    )
    frame = mixed(frame_a, frame_b, weights, subband_ref[...], scratch)
    field = synthesis(frame, block_diagonal(lat_s_ref), both(lon_s_ref))
    for g in range(8):
        channels = slice(4 * g, 4 * g + 4)
        out_ref[channels] = skip_ref[channels] + field[:, 128 * g : 128 * g + 128].reshape(
            4, 64, 128
        )


def full_spec(shape):
    return pl.BlockSpec(shape, lambda *_: (0,) * len(shape))


def part_spec(shape):
    return pl.BlockSpec(shape, lambda _, part: (part[0],) + (0,) * (len(shape) - 1))


def shape_of(*shape, dtype=F32):
    return jax.ShapeDtypeStruct(shape, dtype)


FRAME = pltpu.VMEM((512, 128), F32)


def call(kernel, outs, args, part=None, by_part=(), scratch=()):
    in_specs = [
        part_spec((1,) + arg.shape[1:]) if i in by_part else full_spec(arg.shape)
        for i, arg in enumerate(args)
    ]
    out_specs = [full_spec(out.shape) for out in outs]
    params = pltpu.CompilerParams(vmem_limit_bytes=48 * 1024 * 1024)
    if part is None:
        return pl.pallas_call(
            kernel,
            grid=(1,),
            in_specs=in_specs,
            out_specs=out_specs,
            out_shape=list(outs),
            scratch_shapes=list(scratch),
            compiler_params=params,
        )(*args)
    grid_spec = pltpu.PrefetchScalarGridSpec(
        num_scalar_prefetch=1,
        grid=(1,),
        in_specs=in_specs,
        out_specs=out_specs,
        scratch_shapes=list(scratch),
    )
    return pl.pallas_call(
        kernel, grid_spec=grid_spec, out_shape=list(outs), compiler_params=params
    )(part, *args)


TILE = shape_of(32, 8, 128)
FAR = shape_of(32, 2, 128)
FIELD = shape_of(32, 64, 128)


def exchange(a, b, far, part, subbands, before):
    near = lax.ppermute(a, "lat", [(i, i ^ 1) for i in range(LAT_PARTS)])
    other = lax.ppermute(b, "lat", [(1, 2), (2, 1)])
    far = lax.ppermute(far, "lat", [(i, i ^ 2) for i in range(LAT_PARTS)])
    (near, other, far), before = lax.optimization_barrier(((near, other, far), before))
    fa, fb, low, high = call(
        lat_sum_kernel,
        (TILE,) * 4,
        (jnp.asarray(OWN), a, b, near, other, far, subbands),
        part,
        (0,),
    )
    count = lax.axis_size("lon")
    from_left = lax.ppermute(high, "lon", [(i, (i + 1) % count) for i in range(count)])
    from_right = lax.ppermute(low, "lon", [((i + 1) % count, i) for i in range(count)])
    return (fa, fb, from_left, from_right), before


def swapped(values, axis, distance):
    count = lax.axis_size(axis)
    return lax.ppermute(values, axis, [(i, i ^ distance) for i in range(count)])


def total(values):
    values = values + swapped(values, "lat", 1)
    for distance in (4, 16):
        steps = [swapped(values, "lon", distance * k) for k in (1, 3, 2)]
        values = values + steps[0] + (steps[1] + steps[2])
    values = values + swapped(values, "lon", 1)
    count = lax.axis_size("lon")
    pairs = [
        (4 * lon + lat, 4 * (lon ^ 2) + (lat ^ 2)) for lon in range(count) for lat in range(4)
    ]
    steps = (
        swapped(values, "lon", 2),
        lax.ppermute(values, ("lon", "lat"), pairs),
        swapped(values, "lat", 2),
    )
    return values + steps[0] + (steps[1] + steps[2])


def on_device(ocean_field, cotangent, mix_coarse, mix_detail, skip_weight, bias_vector):
    part = lax.axis_index("lat").astype(jnp.int32).reshape(1)
    lat_a, lat_s = jnp.asarray(LAT_A), jnp.asarray(LAT_S)
    lon_a, lon_s = jnp.asarray(LON_A), jnp.asarray(LON_S)
    subbands = jnp.asarray(SUBBANDS)
    a, b, far = call(
        analysis_kernel, (TILE, TILE, FAR), (ocean_field, lat_a, lon_a), part, (1,)
    )
    (pre,) = call(skip_kernel, (FIELD,), (ocean_field, skip_weight, bias_vector.reshape(1, 32)))
    shares, pre = exchange(a, b, far, part, subbands, pre)
    activated, grad_pre, coef_a, coef_b, a, b, far = call(
        forward_kernel,
        (shape_of(32, 64, 128, dtype=BF16), FIELD, TILE, TILE, TILE, TILE, FAR),
        (*shares, pre, cotangent, mix_coarse, mix_detail, subbands, lat_a, lat_s, lon_a, lon_s),
        part,
        (9, 10),
        (FRAME,),
    )
    (sums,) = call(
        weights_kernel,
        (shape_of(72, 128),),
        (ocean_field, grad_pre, coef_a, coef_b, a, b, subbands),
        scratch=(FRAME, FRAME),
    )
    (skip_back,) = call(skip_back_kernel, (FIELD,), (grad_pre, skip_weight))
    shares, skip_back = exchange(a, b, far, part, subbands, skip_back)
    (grad_field,) = call(
        backward_kernel,
        (FIELD,),
        (*shares, skip_back, mix_coarse, mix_detail, subbands, lat_s, lon_s),
        part,
        (8,),
        (FRAME,),
    )
    cells = LAT_PARTS * LAT_BLOCK * LON_BLOCK * lax.axis_size("lon")
    coarse, detail, grad_skip, grad_bias = call(
        functools.partial(result_kernel, cells=cells),
        (shape_of(4, 32, 32), shape_of(3, 32, 32), shape_of(32, 32), shape_of(1, 32)),
        (total(sums),),
    )
    return (activated, grad_field, coarse, detail, grad_skip, grad_bias.reshape(32))


def solution(mesh):
    return jax.shard_map(
        on_device,
        mesh=mesh,
        in_specs=(P(None, "lat", "lon"), P(None, "lat", "lon"), P(), P(), P(), P()),
        out_specs=(P(None, "lat", "lon"), P(None, "lat", "lon"), P(), P(), P(), P()),
        check_vma=False,
    )
```

```python
import functools
import math

import jax
import jax.numpy as jnp
import numpy as np
from jax import lax
from jax.experimental import pallas as pl
from jax.experimental.pallas import tpu as pltpu
from jax.sharding import PartitionSpec as P
from ml_dtypes import bfloat16

F32 = jnp.float32
BF16 = jnp.bfloat16

low_taps = (
    -0.010597401785069032,
    0.0328830116668852,
    0.030841381835560764,
    -0.18703481171909309,
    -0.027983769416859854,
    0.6308807679298589,
    0.7148465705529157,
    0.2303778133088965,
)
high_taps = (
    -0.2303778133088965,
    0.7148465705529157,
    -0.6308807679298589,
    -0.027983769416859854,
    0.18703481171909309,
    0.030841381835560764,
    -0.0328830116668852,
    -0.010597401785069032,
)

CHANNELS = 32
LAT_PARTS = 4
LAT_BLOCK = 64
LON_BLOCK = 128
LAT_BAND = (0, 1, 0, 1, 3, 2, 3)
LON_BAND = (0, 0, 1, 1, 2, 3, 3)
LO_LANES = 42
HI_LANE = 64


def level_matrix(size, taps, periodic):
    matrix = np.zeros((size // 2, size))
    for k in range(size // 2):
        for j in range(8):
            m = 2 * k + j - 3
            if periodic:
                matrix[k, m % size] += taps[j]
            elif 0 <= m < size:
                matrix[k, m] += taps[j]
    return matrix


def composed(size, periodic):
    two = level_matrix(size // 2, low_taps, periodic) @ level_matrix(size, low_taps, periodic)
    three_low = level_matrix(size // 4, low_taps, periodic) @ two
    three_high = level_matrix(size // 4, high_taps, periodic) @ two
    four_low = level_matrix(size // 8, low_taps, periodic) @ three_low
    four_high = level_matrix(size // 8, high_taps, periodic) @ three_low
    return (four_low, four_high, three_low, three_high)


def lane_table():
    lanes = [None] * 128
    inner = []
    for s in range(7):
        count = 14 if s < 4 else 22
        for e in range(6):
            lanes[s * 6 + e] = (s, e)
            lanes[HI_LANE + s * 6 + e] = (s, count - 6 + e)
        inner += [(s, e) for e in range(6, count - 6)]
    free = [lane for lane in range(128) if lanes[lane] is None]
    for lane, entry in zip(free, inner):
        lanes[lane] = entry
    return lanes


LANES = lane_table()
SUBBAND_OF_LANE = np.array([-1 if entry is None else entry[0] for entry in LANES])


def lon_weights():
    maps = composed(8 * LON_BLOCK, True)
    start = 3 * LON_BLOCK
    weights = np.zeros((4, LON_BLOCK, 128))
    for lane, entry in enumerate(LANES):
        if entry is None:
            continue
        s, e = entry
        per_block = 8 if s < 4 else 16
        row = maps[LON_BAND[s]][3 * per_block - 3 + e]
        weights[LAT_BAND[s], :, lane] = row[start : start + LON_BLOCK]
    return weights.reshape(4 * LON_BLOCK, 128)


def row_entries(part):
    top4, bottom4 = list(range(6)) + [None] * 2, list(range(4, 10)) + [None] * 2
    top3, bottom3 = list(range(8)), list(range(8, 14)) + [None] * 2
    four = bottom4 + top4 if part % 2 == 0 else top4 + bottom4
    three = bottom3 + top3 if part % 2 == 0 else top3 + bottom3
    four[14:16] = [8, 9] if part < 2 else [0, 1]
    return four, three


def lat_weights():
    maps = composed(LAT_PARTS * LAT_BLOCK, False)
    weights = np.zeros((LAT_PARTS, 4, 16, LAT_BLOCK))
    for part in range(LAT_PARTS):
        entries = row_entries(part)
        for band in range(4):
            per_block = 4 if band < 2 else 8
            for row, e in enumerate(entries[0 if band < 2 else 1]):
                k = per_block * part - 3 + e if e is not None else -1
                if 0 <= k < per_block * LAT_PARTS:
                    weights[part, band, row] = maps[band][
                        k, part * LAT_BLOCK : (part + 1) * LAT_BLOCK
                    ]
    return weights.reshape(LAT_PARTS, 64, LAT_BLOCK)


def own_mask():
    mask = np.ones((LAT_PARTS, 16, 128), np.float32)
    four = (SUBBAND_OF_LANE >= 0) & (SUBBAND_OF_LANE < 4)
    for part in range(LAT_PARTS):
        bottom = 0 if part % 2 == 0 else 8
        for row in (bottom, bottom + 1, 14, 15):
            mask[part, row, four] = 0.0
    return mask


def high_low(matrix):
    matrix = matrix.astype(np.float32)
    high = matrix.astype(bfloat16)
    low = (matrix - high.astype(np.float32)).astype(bfloat16)
    return np.stack([high, low], axis=-3)


LON = lon_weights()
LAT = lat_weights()
LON_ROWS = 1024


def packed(lon, lat):
    lon = high_low(lon)
    lon = np.concatenate(
        [lon[:, :, 128 * b : 128 * b + 128] for b in range(lon.shape[2] // 128)], axis=1
    )
    lat = high_low(np.tile(lat, (1, 1, 2)))
    return np.concatenate([lon.reshape(LON_ROWS, 128), lat.reshape(-1, 128)])


ANALYSIS = packed(LON, LAT)
SYNTHESIS = packed(LON.T, LAT.transpose(0, 2, 1))
OWN = own_mask()
SUBBANDS = np.tile(SUBBAND_OF_LANE.astype(np.float32), (8, 1))


def split(x):
    high = x.astype(BF16)
    low = (x - high.astype(F32)).astype(BF16)
    return high, low


def dot(a, b):
    return jnp.dot(a, b, preferred_element_type=F32)


def dot_nt(a, b):
    return lax.dot_general(a, b, (((1,), (1,)), ((), ())), preferred_element_type=F32)


def dot3(a, b, product=dot):
    return product(a[0], b[0]) + (product(a[0], b[1]) + product(a[1], b[0]))


def lat_matrix(table_ref, part):
    row = lax.broadcasted_iota(jnp.int32, (256, 256), 0)
    keep = row // 64 == lane_index((256, 256)) // 64
    first = pl.multiple_of(LON_ROWS + 128 * part, 128)
    block = table_ref[pl.ds(first, 128), :]
    return tuple(
        jnp.where(keep, jnp.tile(block[64 * k : 64 * k + 64], (4, 2)), 0.0).astype(BF16)
        for k in range(2)
    )


def lon_analysis(table_ref):
    return table_ref[0:512], table_ref[512:1024]


def lon_synthesis(table_ref):
    return tuple(
        jnp.concatenate(
            [table_ref[512 * k + 128 * b : 512 * k + 128 * b + 128] for b in range(4)], axis=1
        )
        for k in range(2)
    )


def lat_part(part_ref):
    return part_ref[0] // 2


def is_even(part_ref):
    return part_ref[0] % 2 == 0


def grouped(x):
    return jnp.concatenate(
        [x[4 * g : 4 * g + 4].reshape(256, 128) for g in range(x.shape[0] // 4)], axis=1
    )


def tiled(x):
    return jnp.concatenate(
        [x[:, 8 * t : 8 * t + 8, :].reshape(256, 128) for t in range(8)], axis=1
    )


def analysis(groups, lat, lon):
    rows = dot3(lat, split(groups))
    count = groups.shape[1] // 128
    blocks = []
    for g in range(count):
        part = rows[:, 128 * g : 128 * g + 128].reshape(4, 4, 16, 128)
        blocks.append(
            jnp.concatenate([part[:, b].reshape(64, 128) for b in range(4)], axis=1)
        )
    return dot3(split(jnp.concatenate(blocks, axis=0)), lon).reshape(4 * count, 16, 128)


def synthesis_rows(frame, lon):
    wide = dot3(split(frame), lon).reshape(8, 4, 16, 512)
    groups = []
    for g in range(8):
        part = jnp.stack(
            [wide[g, :, :, 128 * b : 128 * b + 128] for b in range(4)], axis=1
        )
        groups.append(part.reshape(256, 128))
    return jnp.concatenate(groups, axis=1)


def lane_index(shape):
    return lax.broadcasted_iota(jnp.int32, shape, len(shape) - 1)


def rolled(x, shift):
    return pltpu.roll(x, shift % 128, 2) if shift % 128 else x


def edge_lanes(frame, first):
    lane = lane_index((11, 16, 128))
    parts = [rolled(frame[c : c + 11], LO_LANES * k - first) for k, c in enumerate((0, 11, 21))]
    return jnp.where(
        lane < LO_LANES, parts[0], jnp.where(lane < 2 * LO_LANES, parts[1], parts[2])
    )


def placed_lanes(edge, first):
    parts = [rolled(edge, first - LO_LANES * k) for k in range(3)]
    whole = jnp.concatenate([parts[0], parts[1], parts[2][1:]], axis=0)
    lane = lane_index(whole.shape)
    return jnp.where((lane >= first) & (lane < first + LO_LANES), whole, 0.0)


def add_edges(frame_ref, even, first, second):
    from_left = jnp.where(even, first, second)
    from_right = jnp.where(even, second, first)
    added = placed_lanes(from_left, 0) + placed_lanes(from_right, HI_LANE)
    return frame_ref[...] + added.reshape(512, 128)


def by_row(frame_ref):
    return jnp.concatenate([frame_ref[pl.ds(r, 32, stride=16), :] for r in range(16)], axis=1)


def stacked(data, subbands):
    lanes = jnp.concatenate([subbands[0:1]] * 16, axis=1)
    return [
        jnp.concatenate(
            [jnp.where(lanes == float(s), part, 0.0).astype(BF16) for s in range(7)], axis=0
        )
        for part in (data, data - data.astype(BF16).astype(F32))
    ]


def mixed(frame_ref, weights, subbands, scratch):
    data = stacked(by_row(frame_ref), subbands)
    high, low = split(weights)
    double = dot(jnp.concatenate([high, low], axis=0), data[0])
    result = double[:32] + (double[32:] + dot(high, data[1]))
    for r in range(16):
        scratch[pl.ds(r, 32, stride=16), :] = result[:, 128 * r : 128 * r + 128]
    return scratch[...]


def store_frame(frame, frame_ref, near_ref, other_ref, far_ref):
    frame_ref[...] = frame.reshape(512, 128)
    for target, first, rows in ((near_ref, 0, 6), (other_ref, 8, 6), (far_ref, 14, 2)):
        for r in range(rows):
            target[32 * r : 32 * r + 32] = frame_ref[pl.ds(first + r, 32, stride=16), :]


def analysis_kernel(part_ref, x_ref, table_ref, frame_ref, near_ref, other_ref, far_ref):
    lat = lat_matrix(table_ref, lat_part(part_ref))
    frame = analysis(grouped(x_ref[...]), lat, lon_analysis(table_ref))
    store_frame(frame, frame_ref, near_ref, other_ref, far_ref)


def expand_matrix():
    row = lax.broadcasted_iota(jnp.int32, (256, 32), 0)
    return (row // 8 == lane_index((256, 32))).astype(BF16)


def same_row(shape):
    row = lax.broadcasted_iota(jnp.int32, shape, 0)
    return lax.rem(row, 8) == lax.rem(lane_index(shape), 8)


def expanded(weight, product):
    expand = expand_matrix()
    diagonal = same_row((256, 256))
    return tuple(
        jnp.where(diagonal, dot_nt(product(expand, part).astype(BF16), expand), 0.0).astype(BF16)
        for part in split(weight)
    )


def skip_kernel(x_ref, skip_ref, bias_ref, pre_ref):
    weight = expanded(skip_ref[...], dot_nt)
    product = dot3(weight, split(tiled(x_ref[...])))
    bias = jnp.sum(expand_matrix().astype(F32) * bias_ref[...], axis=1, keepdims=True)
    for t in range(8):
        pre_ref[:, 8 * t : 8 * t + 8, :] = (
            product[:, 128 * t : 128 * t + 128] + bias
        ).reshape(32, 8, 128)


def lat_sum_kernel(
    part_ref,
    mask_ref,
    frame_ref,
    near_ref,
    other_ref,
    far_ref,
    subband_ref,
    sum_ref,
    first_ref,
    second_ref,
    *,
    far_row,
):
    frame = frame_ref[...].reshape(32, 16, 128) * mask_ref[0][None]
    sum_ref[...] = frame.reshape(512, 128)
    subband = subband_ref[0:1]
    four = (subband >= 0.0) & (subband < 4.0)
    for r in range(6):
        sum_ref[pl.ds(r, 32, stride=16), :] += near_ref[32 * r : 32 * r + 32]
        sum_ref[pl.ds(8 + r, 32, stride=16), :] += other_ref[32 * r : 32 * r + 32]
    for r in range(2):
        far = far_ref[far_row + 32 * r : far_row + 32 * r + 32]
        sum_ref[pl.ds(14 + r, 32, stride=16), :] += jnp.where(four, far, 0.0)
    frame = sum_ref[...].reshape(32, 16, 128)
    low, high = edge_lanes(frame, 0), edge_lanes(frame, HI_LANE)
    even = is_even(part_ref)
    first_ref[...] = jnp.where(even, low, high)
    second_ref[...] = jnp.where(even, high, low)


def forward_kernel(
    part_ref,
    shares_ref,
    first_ref,
    second_ref,
    pre_ref,
    cot_ref,
    coarse_ref,
    detail_ref,
    subband_ref,
    analysis_ref,
    synthesis_ref,
    act_ref,
    grad_ref,
    coef_ref,
    frame_ref,
    near_ref,
    other_ref,
    far_ref,
    scratch,
    act,
    done,
):
    coef_ref[...] = add_edges(
        shares_ref, is_even(part_ref), first_ref[...], second_ref[...]
    )
    weights = jnp.concatenate(
        [coarse_ref[s].T for s in range(4)] + [detail_ref[s].T for s in range(3)], axis=1
    )
    frame = mixed(coef_ref, weights, subband_ref[...], scratch)
    rows = synthesis_rows(frame, lon_synthesis(synthesis_ref))
    lat = lat_matrix(synthesis_ref, lat_part(part_ref))
    grads = []
    stores = []
    for q in range(4):
        kernel = dot3(lat, split(rows[:, 256 * q : 256 * q + 256]))
        for g in (2 * q, 2 * q + 1):
            channels = slice(4 * g, 4 * g + 4)
            lanes = slice(128 * (g - 2 * q), 128 * (g - 2 * q) + 128)
            pre = kernel[:, lanes] + pre_ref[channels].reshape(256, 128)
            cumulative = 0.5 * (1.0 + lax.erf(pre * math.sqrt(0.5)))
            density = jnp.exp(-0.5 * pre * pre) * (1.0 / math.sqrt(2.0 * math.pi))
            act[channels] = (pre * cumulative).astype(BF16).reshape(4, 64, 128)
            grad = cot_ref[channels].astype(F32).reshape(256, 128) * (cumulative + pre * density)
            grad_ref[channels] = grad.reshape(4, 64, 128)
            grads.append(grad)
        block = pl.ds(8 * q, 8)
        stores.append(pltpu.make_async_copy(act.at[block], act_ref.at[block], done.at[q]))
        stores[q].start()
    frame = analysis(
        jnp.concatenate(grads, axis=1),
        lat_matrix(analysis_ref, lat_part(part_ref)),
        lon_analysis(analysis_ref),
    )
    store_frame(frame, frame_ref, near_ref, other_ref, far_ref)
    for store in stores:
        store.wait()


def weights_kernel(x_ref, g_ref, coef_ref, frame_ref, near_ref, subband_ref, sum_ref):
    def placed(parts, offset):
        row = lax.broadcasted_iota(jnp.int32, (256, 128), 0)
        place = (row // 8 + offset == lane_index((256, 128))).astype(BF16)
        return dot(parts[0], place) + dot(parts[1], place)

    coef = stacked(by_row(coef_ref), subband_ref[...])
    high, low = split(by_row(frame_ref))
    double = dot_nt(jnp.concatenate([high, low], axis=0), coef[0])
    mix = double[:32] + (double[32:] + dot_nt(high, coef[1]))
    mix = jnp.concatenate([mix, jnp.zeros((32, 32), F32)], axis=1)
    field = split(tiled(x_ref[...]))
    grad_pre = split(tiled(g_ref[...]))
    product = jnp.where(same_row((256, 256)), dot3(grad_pre, field, dot_nt), 0.0)
    skip = split(jnp.sum(product.reshape(32, 8, 256), axis=1))
    ones = jnp.ones((8, 1024), BF16)
    bias = split(dot_nt(ones, grad_pre[0]) + dot_nt(ones, grad_pre[1]))
    sum_ref[0:192] = near_ref[...]
    sum_ref[192:224] = mix[:, :128]
    sum_ref[224:256] = mix[:, 128:] + placed(skip, 96)
    sum_ref[256:264] = placed(bias, 0)


def pair_kernel(own_ref, near_ref, far_ref, out_ref):
    out_ref[0:72] = own_ref[192:264] + near_ref[192:264]
    out_ref[72:136] = far_ref[...]


def result_kernel(sum_ref, coarse_ref, detail_ref, skip_ref, bias_ref, cells):
    first = sum_ref[0:32].T
    second = sum_ref[32:64].T
    for s in range(4):
        coarse_ref[s] = first[32 * s : 32 * s + 32] * (1.0 / math.sqrt(cells // 256))
    for s in range(3):
        detail_ref[s] = second[32 * s : 32 * s + 32] * (1.0 / math.sqrt(cells // 64))
    skip_ref[...] = second[96:] * (1.0 / math.sqrt(cells))
    bias_ref[...] = sum_ref[64:65, :32] * (1.0 / math.sqrt(cells))


def skip_back_kernel(g_ref, skip_ref, out_ref):
    product = dot3(expanded(skip_ref[...], dot), split(tiled(g_ref[...])))
    for t in range(8):
        out_ref[:, 8 * t : 8 * t + 8, :] = product[:, 128 * t : 128 * t + 128].reshape(32, 8, 128)


def backward_kernel(
    part_ref,
    shares_ref,
    first_ref,
    second_ref,
    skip_ref,
    coarse_ref,
    detail_ref,
    subband_ref,
    synthesis_ref,
    out_ref,
    whole,
    scratch,
    field,
    done,
):
    whole[...] = add_edges(shares_ref, is_even(part_ref), first_ref[...], second_ref[...])
    weights = jnp.concatenate(
        [coarse_ref[s] for s in range(4)] + [detail_ref[s] for s in range(3)], axis=1
    )
    frame = mixed(whole, weights, subband_ref[...], scratch)
    rows = synthesis_rows(frame, lon_synthesis(synthesis_ref))
    lat = lat_matrix(synthesis_ref, lat_part(part_ref))
    stores = []
    for q in range(4):
        part = dot3(lat, split(rows[:, 256 * q : 256 * q + 256]))
        for g in (2 * q, 2 * q + 1):
            channels = slice(4 * g, 4 * g + 4)
            lanes = slice(128 * (g - 2 * q), 128 * (g - 2 * q) + 128)
            field[channels] = skip_ref[channels] + part[:, lanes].reshape(4, 64, 128)
        block = pl.ds(8 * q, 8)
        stores.append(pltpu.make_async_copy(field.at[block], out_ref.at[block], done.at[q]))
        stores[q].start()
    for store in stores:
        store.wait()


def full_spec(shape):
    return pl.BlockSpec(shape, lambda *_: (0,) * len(shape))


def part_spec(shape):
    return pl.BlockSpec(shape, lambda _, part: (part[0] // 2,) + (0,) * (len(shape) - 1))


def shape_of(*shape, dtype=F32):
    return jax.ShapeDtypeStruct(shape, dtype)


FRAME = pltpu.VMEM((512, 128), F32)


def call(kernel, outs, args, part=None, by_part=(), scratch=(), in_hbm=()):
    in_specs = [
        part_spec((1,) + arg.shape[1:]) if i in by_part else full_spec(arg.shape)
        for i, arg in enumerate(args)
    ]
    out_specs = [
        pl.BlockSpec(memory_space=pltpu.HBM) if i in in_hbm else full_spec(out.shape)
        for i, out in enumerate(outs)
    ]
    params = pltpu.CompilerParams(vmem_limit_bytes=48 * 1024 * 1024)
    if part is None:
        return pl.pallas_call(
            kernel,
            grid=(1,),
            in_specs=in_specs,
            out_specs=out_specs,
            out_shape=list(outs),
            scratch_shapes=list(scratch),
            compiler_params=params,
        )(*args)
    grid_spec = pltpu.PrefetchScalarGridSpec(
        num_scalar_prefetch=1,
        grid=(1,),
        in_specs=in_specs,
        out_specs=out_specs,
        scratch_shapes=list(scratch),
    )
    return pl.pallas_call(
        kernel, grid_spec=grid_spec, out_shape=list(outs), compiler_params=params
    )(part, *args)


COEFS = shape_of(512, 128)
ROWS = shape_of(192, 128)
FAR = shape_of(64, 128)
EDGE = shape_of(11, 16, 128)
FIELD = shape_of(32, 64, 128)


def swapped(values, axis, distance):
    count = lax.axis_size(axis)
    return lax.ppermute(values, axis, [(i, i ^ distance) for i in range(count)])


def ring(values, unit):
    count = lax.axis_size("lon")
    step = (3, 1, -1, -3)
    return lax.ppermute(
        values, "lon", [(i, i + step[i // unit % 4] * unit) for i in range(count)]
    )


def middle(values):
    return lax.ppermute(values, "lat", [(1, 2), (2, 1)])


def lat_sum(frame, near, other, far, far_row, part, subbands):
    return call(
        functools.partial(lat_sum_kernel, far_row=far_row),
        (COEFS, EDGE, EDGE),
        (jnp.asarray(OWN), frame, near, other, far, subbands),
        part,
        (0,),
    )


def lon_exchange(first, second):
    count = lax.axis_size("lon")
    pairs = [(i, (i - 1 + 2 * (i % 2)) % count) for i in range(count)]
    return lax.ppermute(first, "lon", pairs), swapped(second, "lon", 1)


def after(values, others):
    return lax.optimization_barrier((values, others))[0]


def on_device(ocean_field, cotangent, mix_coarse, mix_detail, skip_weight, bias_vector):
    part = (2 * lax.axis_index("lat") + lax.axis_index("lon") % 2).astype(jnp.int32).reshape(1)
    analysis_table, synthesis_table = jnp.asarray(ANALYSIS), jnp.asarray(SYNTHESIS)
    subbands = jnp.asarray(SUBBANDS)
    frame, near, other, far = call(
        analysis_kernel, (COEFS, ROWS, ROWS, FAR), (ocean_field, analysis_table), part
    )
    (pre,) = call(skip_kernel, (FIELD,), (ocean_field, skip_weight, bias_vector.reshape(1, 32)))
    near = swapped(near, "lat", 1)
    other = middle(other)
    far = swapped(far, "lat", 2)
    (near, other, far), pre = lax.optimization_barrier(((near, other, far), pre))
    shares, first, second = lat_sum(frame, near, other, far, 0, part, subbands)
    first, second = lon_exchange(first, second)
    activated, grad_pre, coef, frame, near, other, far = call(
        forward_kernel,
        (shape_of(32, 64, 128, dtype=BF16), FIELD, COEFS, COEFS, ROWS, ROWS, FAR),
        (
            shares,
            first,
            second,
            pre,
            cotangent,
            mix_coarse,
            mix_detail,
            subbands,
            analysis_table,
            synthesis_table,
        ),
        part,
        scratch=(FRAME, pltpu.VMEM((32, 64, 128), BF16), pltpu.SemaphoreType.DMA((4,))),
        in_hbm=(0,),
    )
    (own,) = call(
        weights_kernel,
        (shape_of(264, 128),),
        (ocean_field, grad_pre, coef, frame, near, subbands),
    )
    near = swapped(own, "lat", 1)
    (pair,) = call(pair_kernel, (shape_of(136, 128),), (own, near, far))
    far = swapped(pair, "lat", 2)
    other = middle(after(other, pair))
    sums = pair[:72] + far[:72]
    (skip_back,) = call(skip_back_kernel, (FIELD,), (grad_pre, skip_weight))
    steps = [swapped(sums, "lon", k) for k in (4, 12, 8)]
    near, steps[0] = lax.optimization_barrier((near, steps[0]))
    shares, first, second = lat_sum(frame, near, other, far, 72, part, subbands)
    first, second = lon_exchange(first, second)
    sums = sums + steps[0] + (steps[1] + steps[2])
    step = swapped(sums, "lon", 16)
    sums, first, second, skip_back = lax.optimization_barrier((sums, first, second, skip_back))
    sums = sums + step + (swapped(sums, "lon", 48) + swapped(sums, "lon", 32))
    steps = [swapped(sums, "lon", k) for k in (1, 3, 2)]
    sums = sums + steps[0] + (steps[1] + steps[2])
    (grad_field,) = call(
        backward_kernel,
        (FIELD,),
        (shares, first, second, skip_back, mix_coarse, mix_detail, subbands, synthesis_table),
        part,
        scratch=(FRAME, FRAME, pltpu.VMEM((32, 64, 128), F32), pltpu.SemaphoreType.DMA((4,))),
        in_hbm=(0,),
    )
    cells = LAT_PARTS * LAT_BLOCK * LON_BLOCK * lax.axis_size("lon")
    coarse, detail, grad_skip, grad_bias = call(
        functools.partial(result_kernel, cells=cells),
        (shape_of(4, 32, 32), shape_of(3, 32, 32), shape_of(32, 32), shape_of(1, 32)),
        (sums,),
    )
    return (activated, grad_field, coarse, detail, grad_skip, grad_bias.reshape(32))


def solution(mesh):
    return jax.shard_map(
        on_device,
        mesh=mesh,
        in_specs=(P(None, "lat", "lon"), P(None, "lat", "lon"), P(), P(), P(), P()),
        out_specs=(P(None, "lat", "lon"), P(None, "lat", "lon"), P(), P(), P(), P()),
        check_vma=False,
    )
```

```python
import functools
import math

import jax
import jax.numpy as jnp
import numpy as np
from jax import lax
from jax.experimental import pallas as pl
from jax.experimental.pallas import tpu as pltpu
from jax.sharding import PartitionSpec as P
from ml_dtypes import bfloat16

F32 = jnp.float32
BF16 = jnp.bfloat16

low_taps = (
    -0.010597401785069032,
    0.0328830116668852,
    0.030841381835560764,
    -0.18703481171909309,
    -0.027983769416859854,
    0.6308807679298589,
    0.7148465705529157,
    0.2303778133088965,
)
high_taps = (
    -0.2303778133088965,
    0.7148465705529157,
    -0.6308807679298589,
    -0.027983769416859854,
    0.18703481171909309,
    0.030841381835560764,
    -0.0328830116668852,
    -0.010597401785069032,
)

CHANNELS = 32
LAT_PARTS = 4
LAT_BLOCK = 64
LON_BLOCK = 128
LAT_BAND = (0, 1, 0, 1, 3, 2, 3)
LON_BAND = (0, 0, 1, 1, 2, 3, 3)
LO_LANES = 42
FAR_SHIFT = 32
HI_LANE = 64


def level_matrix(size, taps, periodic):
    matrix = np.zeros((size // 2, size))
    for k in range(size // 2):
        for j in range(8):
            m = 2 * k + j - 3
            if periodic:
                matrix[k, m % size] += taps[j]
            elif 0 <= m < size:
                matrix[k, m] += taps[j]
    return matrix


def composed(size, periodic):
    two = level_matrix(size // 2, low_taps, periodic) @ level_matrix(size, low_taps, periodic)
    three_low = level_matrix(size // 4, low_taps, periodic) @ two
    three_high = level_matrix(size // 4, high_taps, periodic) @ two
    four_low = level_matrix(size // 8, low_taps, periodic) @ three_low
    four_high = level_matrix(size // 8, high_taps, periodic) @ three_low
    return (four_low, four_high, three_low, three_high)


def lane_table():
    lanes = [None] * 128
    coarse_inner, inner = [], []
    for s in range(7):
        count = 14 if s < 4 else 22
        for e in range(6):
            lanes[s * 6 + e] = (s, e)
            lanes[HI_LANE + s * 6 + e] = (s, count - 6 + e)
        target = coarse_inner if s < 4 else inner
        target += [(s, e) for e in range(6, count - 6)]
    lanes[HI_LANE - 8 : HI_LANE] = coarse_inner
    free = [lane for lane in range(128) if lanes[lane] is None]
    for lane, entry in zip(free, inner):
        lanes[lane] = entry
    return lanes


LANES = lane_table()
SUBBAND_OF_LANE = np.array([-1 if entry is None else entry[0] for entry in LANES])


def lon_weights():
    maps = composed(8 * LON_BLOCK, True)
    start = 3 * LON_BLOCK
    weights = np.zeros((4, LON_BLOCK, 128))
    for lane, entry in enumerate(LANES):
        if entry is None:
            continue
        s, e = entry
        per_block = 8 if s < 4 else 16
        row = maps[LON_BAND[s]][3 * per_block - 3 + e]
        weights[LAT_BAND[s], :, lane] = row[start : start + LON_BLOCK]
    return weights.reshape(4 * LON_BLOCK, 128)


def row_entries(part):
    top4, bottom4 = list(range(6)) + [None] * 2, list(range(4, 10)) + [None] * 2
    top3, bottom3 = list(range(8)), list(range(8, 14)) + [None] * 2
    four = bottom4 + top4 if part % 2 == 0 else top4 + bottom4
    three = bottom3 + top3 if part % 2 == 0 else top3 + bottom3
    four[14:16] = [8, 9] if part < 2 else [0, 1]
    return four, three


def lat_weights():
    maps = composed(LAT_PARTS * LAT_BLOCK, False)
    weights = np.zeros((LAT_PARTS, 4, 16, LAT_BLOCK))
    for part in range(LAT_PARTS):
        entries = row_entries(part)
        for band in range(4):
            per_block = 4 if band < 2 else 8
            for row, e in enumerate(entries[0 if band < 2 else 1]):
                k = per_block * part - 3 + e if e is not None else -1
                if 0 <= k < per_block * LAT_PARTS:
                    weights[part, band, row] = maps[band][
                        k, part * LAT_BLOCK : (part + 1) * LAT_BLOCK
                    ]
    return weights.reshape(LAT_PARTS, 64, LAT_BLOCK)


def own_mask():
    mask = np.ones((LAT_PARTS, 16, 128), np.float32)
    four = (SUBBAND_OF_LANE >= 0) & (SUBBAND_OF_LANE < 4)
    for part in range(LAT_PARTS):
        bottom = 0 if part % 2 == 0 else 8
        for row in (bottom, bottom + 1, 14, 15):
            mask[part, row, four] = 0.0
    return mask


def high_low(matrix):
    matrix = matrix.astype(np.float32)
    high = matrix.astype(bfloat16)
    low = (matrix - high.astype(np.float32)).astype(bfloat16)
    return np.stack([high, low], axis=-3)


LON = lon_weights()
LAT = lat_weights()
LON_ROWS = 1024


def packed(lon, lat):
    lon = high_low(lon)
    lon = np.concatenate(
        [lon[:, :, 128 * b : 128 * b + 128] for b in range(lon.shape[2] // 128)], axis=1
    )
    lat = high_low(np.tile(lat, (1, 1, 2)))
    return np.concatenate([lon.reshape(LON_ROWS, 128), lat.reshape(-1, 128)])


ANALYSIS = packed(LON, LAT)
SYNTHESIS = packed(LON.T, LAT.transpose(0, 2, 1))
OWN = own_mask()
SUBBANDS = np.tile(SUBBAND_OF_LANE.astype(np.float32), (8, 1))


def split(x):
    high = x.astype(BF16)
    low = (x - high.astype(F32)).astype(BF16)
    return high, low


def dot(a, b):
    return jnp.dot(a, b, preferred_element_type=F32)


def dot_nt(a, b):
    return lax.dot_general(a, b, (((1,), (1,)), ((), ())), preferred_element_type=F32)


def dot3(a, b, product=dot):
    return product(a[0], b[0]) + (product(a[0], b[1]) + product(a[1], b[0]))


def lat_matrix(block):
    row = lax.broadcasted_iota(jnp.int32, (256, 256), 0)
    keep = row // 64 == lane_index((256, 256)) // 64
    return tuple(
        jnp.where(keep, jnp.tile(block[64 * k : 64 * k + 64], (4, 2)), 0.0).astype(BF16)
        for k in range(2)
    )


def lat_filters(table_ref, part_ref):
    first = pl.multiple_of(LON_ROWS + 128 * lat_part(part_ref), 128)
    return lat_matrix(table_ref[pl.ds(first, 128), :])


def lon_analysis(table_ref):
    return table_ref[0:512], table_ref[512:1024]


def lon_synthesis(table_ref):
    return tuple(
        jnp.concatenate(
            [table_ref[512 * k + 128 * b : 512 * k + 128 * b + 128] for b in range(4)], axis=1
        )
        for k in range(2)
    )


def lat_part(part_ref):
    return part_ref[0] // 2


def is_even(part_ref):
    return part_ref[0] % 2 == 0


def grouped(x):
    return jnp.concatenate(
        [x[4 * g : 4 * g + 4].reshape(256, 128) for g in range(x.shape[0] // 4)], axis=1
    )


def tiled(x):
    return jnp.concatenate(
        [x[:, 8 * t : 8 * t + 8, :].reshape(256, 128) for t in range(8)], axis=1
    )


def analysis(groups, lat, lon):
    rows = dot3(lat, split(groups))
    count = groups.shape[1] // 128
    blocks = []
    for g in range(count):
        part = rows[:, 128 * g : 128 * g + 128].reshape(4, 4, 16, 128)
        blocks.append(
            jnp.concatenate([part[:, b].reshape(64, 128) for b in range(4)], axis=1)
        )
    return dot3(split(jnp.concatenate(blocks, axis=0)), lon).reshape(4 * count, 16, 128)


def synthesis_rows(frame, lon):
    wide = dot3(split(frame), lon).reshape(-1, 4, 16, 512)
    groups = []
    for g in range(wide.shape[0]):
        part = jnp.stack(
            [wide[g, :, :, 128 * b : 128 * b + 128] for b in range(4)], axis=1
        )
        groups.append(part.reshape(256, 128))
    return jnp.concatenate(groups, axis=1)


def lane_index(shape):
    return lax.broadcasted_iota(jnp.int32, shape, len(shape) - 1)


def rolled(x, shift):
    return pltpu.roll(x, shift % 128, 2) if shift % 128 else x


def edge_lanes(frame, first):
    lane = lane_index((11, 16, 128))
    parts = [rolled(frame[c : c + 11], LO_LANES * k - first) for k, c in enumerate((0, 11, 21))]
    return jnp.where(
        lane < LO_LANES, parts[0], jnp.where(lane < 2 * LO_LANES, parts[1], parts[2])
    )


def placed_lanes(edge, first):
    parts = [rolled(edge, first - LO_LANES * k) for k in range(3)]
    whole = jnp.concatenate([parts[0], parts[1], parts[2][1:]], axis=0)
    lane = lane_index(whole.shape)
    return jnp.where((lane >= first) & (lane < first + LO_LANES), whole, 0.0)


def add_edges(frame_ref, even, first, second):
    from_left = jnp.where(even, first, second)
    from_right = jnp.where(even, second, first)
    added = placed_lanes(from_left, 0) + placed_lanes(from_right, HI_LANE)
    return frame_ref[...] + added.reshape(512, 128)


def by_row(frame_ref):
    return jnp.concatenate([frame_ref[pl.ds(r, 32, stride=16), :] for r in range(16)], axis=1)


def stacked(data, subbands):
    masks = [
        jnp.concatenate([(subbands[0:1] == float(s)).astype(BF16)] * 16, axis=1) for s in range(7)
    ]
    return [jnp.concatenate([part * mask for mask in masks], axis=0) for part in split(data)]


def mixed(frame_ref, weights, subbands, scratch):
    data = stacked(by_row(frame_ref), subbands)
    high, low = split(weights)
    double = dot(jnp.concatenate([high, low], axis=0), data[0])
    result = double[:32] + (double[32:] + dot(high, data[1]))
    for r in range(16):
        scratch[pl.ds(r, 32, stride=16), :] = result[:, 128 * r : 128 * r + 128]
    return scratch[...]


def coarse_lanes():
    lane = lane_index((1, 128))
    return (lane < 24) | ((lane >= HI_LANE - 8) & (lane < HI_LANE + 24))


def store_frame(frame, frame_ref, near_ref, other_ref):
    frame_ref[...] = frame.reshape(512, 128)
    for target, first in ((near_ref, 0), (other_ref, 8)):
        for r in range(6):
            target[32 * r : 32 * r + 32] = frame_ref[pl.ds(first + r, 32, stride=16), :]


def far_rows(frame_ref):
    coarse = coarse_lanes()
    rows = [jnp.where(coarse, frame_ref[pl.ds(14 + r, 32, stride=16), :], 0.0) for r in range(2)]
    return rows[0] + pltpu.roll(rows[1], FAR_SHIFT, 1)


def analysis_kernel(part_ref, x_ref, table_ref, frame_ref, near_ref, other_ref, far_ref):
    lat = lat_filters(table_ref, part_ref)
    frame = analysis(grouped(x_ref[...]), lat, lon_analysis(table_ref))
    store_frame(frame, frame_ref, near_ref, other_ref)
    far_ref[...] = far_rows(frame_ref)


def expand_matrix():
    row = lax.broadcasted_iota(jnp.int32, (256, 32), 0)
    return (row // 8 == lane_index((256, 32))).astype(BF16)


def same_row(shape):
    row = lax.broadcasted_iota(jnp.int32, shape, 0)
    return lax.rem(row, 8) == lax.rem(lane_index(shape), 8)


def expanded(weight, product):
    expand = expand_matrix()
    diagonal = same_row((256, 256))
    return tuple(
        jnp.where(diagonal, dot_nt(product(expand, part).astype(BF16), expand), 0.0).astype(BF16)
        for part in split(weight)
    )


def skip_kernel(x_ref, skip_ref, bias_ref, pre_ref):
    weight = expanded(skip_ref[...], dot_nt)
    product = dot3(weight, split(tiled(x_ref[...])))
    bias = jnp.sum(expand_matrix().astype(F32) * bias_ref[...], axis=1, keepdims=True)
    for t in range(8):
        pre_ref[:, 8 * t : 8 * t + 8, :] = (
            product[:, 128 * t : 128 * t + 128] + bias
        ).reshape(32, 8, 128)


def lat_sum_kernel(
    part_ref,
    mask_ref,
    frame_ref,
    near_ref,
    other_ref,
    far_ref,
    sum_ref,
    first_ref,
    second_ref,
    *,
    far_row,
):
    frame = frame_ref[...].reshape(32, 16, 128) * mask_ref[0][None]
    sum_ref[...] = frame.reshape(512, 128)
    coarse = coarse_lanes()
    for r in range(6):
        sum_ref[pl.ds(r, 32, stride=16), :] += near_ref[32 * r : 32 * r + 32]
        sum_ref[pl.ds(8 + r, 32, stride=16), :] += other_ref[32 * r : 32 * r + 32]
    far = far_ref[far_row : far_row + 32]
    for r, shared in enumerate((far, pltpu.roll(far, 128 - FAR_SHIFT, 1))):
        sum_ref[pl.ds(14 + r, 32, stride=16), :] += jnp.where(coarse, shared, 0.0)
    frame = sum_ref[...].reshape(32, 16, 128)
    low, high = edge_lanes(frame, 0), edge_lanes(frame, HI_LANE)
    even = is_even(part_ref)
    first_ref[...] = jnp.where(even, low, high)
    second_ref[...] = jnp.where(even, high, low)


def forward_kernel(
    part_ref,
    shares_ref,
    first_ref,
    second_ref,
    pre_ref,
    cot_ref,
    coarse_ref,
    detail_ref,
    subband_ref,
    analysis_ref,
    synthesis_ref,
    act_ref,
    grad_ref,
    coef_ref,
    frame_ref,
    near_ref,
    other_ref,
    scratch,
    act,
    done,
):
    coef_ref[...] = add_edges(
        shares_ref, is_even(part_ref), first_ref[...], second_ref[...]
    )
    weights = jnp.concatenate(
        [coarse_ref[s].T for s in range(4)] + [detail_ref[s].T for s in range(3)], axis=1
    )
    frame = mixed(coef_ref, weights, subband_ref[...], scratch)
    lon = lon_synthesis(synthesis_ref)
    lat = lat_filters(synthesis_ref, part_ref)
    grads = []
    stores = []
    for q in range(4):
        kernel = dot3(lat, split(synthesis_rows(frame[128 * q : 128 * q + 128], lon)))
        for g in (2 * q, 2 * q + 1):
            channels = slice(4 * g, 4 * g + 4)
            lanes = slice(128 * (g - 2 * q), 128 * (g - 2 * q) + 128)
            pre = kernel[:, lanes] + pre_ref[channels].reshape(256, 128)
            cumulative = 0.5 * (1.0 + lax.erf(pre * math.sqrt(0.5)))
            density = jnp.exp(-0.5 * pre * pre) * (1.0 / math.sqrt(2.0 * math.pi))
            act[channels] = (pre * cumulative).astype(BF16).reshape(4, 64, 128)
            grad = cot_ref[channels].astype(F32).reshape(256, 128) * (cumulative + pre * density)
            grad_ref[channels] = grad.reshape(4, 64, 128)
            grads.append(grad)
        block = pl.ds(8 * q, 8)
        stores.append(pltpu.make_async_copy(act.at[block], act_ref.at[block], done.at[q]))
        stores[q].start()
    frame = analysis(
        jnp.concatenate(grads, axis=1),
        lat_filters(analysis_ref, part_ref),
        lon_analysis(analysis_ref),
    )
    store_frame(frame, frame_ref, near_ref, other_ref)
    for store in stores:
        store.wait()


def weights_kernel(x_ref, g_ref, coef_ref, frame_ref, near_ref, subband_ref, sum_ref):
    def placed(parts, offset):
        row = lax.broadcasted_iota(jnp.int32, (256, 128), 0)
        place = (row // 8 + offset == lane_index((256, 128))).astype(BF16)
        return dot(parts[0], place) + dot(parts[1], place)

    coef = stacked(by_row(coef_ref), subband_ref[...])
    high, low = split(by_row(frame_ref))
    double = dot_nt(jnp.concatenate([high, low], axis=0), coef[0])
    mix = double[:32] + (double[32:] + dot_nt(high, coef[1]))
    mix = jnp.concatenate([mix, jnp.zeros((32, 32), F32)], axis=1)
    field = split(tiled(x_ref[...]))
    grad_pre = split(tiled(g_ref[...]))
    product = jnp.where(same_row((256, 256)), dot3(grad_pre, field, dot_nt), 0.0)
    skip = split(jnp.sum(product.reshape(32, 8, 256), axis=1))
    rows = split(jnp.sum(g_ref[...].reshape(32, 8, 8, 128), axis=1).reshape(256, 128))
    ones = jnp.ones((8, 128), BF16)
    bias = split(dot_nt(ones, rows[0]) + dot_nt(ones, rows[1]))
    sum_ref[0:192] = near_ref[...]
    sum_ref[192:224] = mix[:, :128]
    sum_ref[224:256] = mix[:, 128:] + placed(skip, 96)
    sum_ref[256:264] = placed(bias, 0)


def pair_kernel(own_ref, near_ref, frame_ref, out_ref):
    out_ref[0:72] = own_ref[192:264] + near_ref[192:264]
    out_ref[72:104] = far_rows(frame_ref)


def result_kernel(sum_ref, coarse_ref, detail_ref, skip_ref, bias_ref, cells):
    first = sum_ref[0:32].T
    second = sum_ref[32:64].T
    for s in range(4):
        coarse_ref[s] = first[32 * s : 32 * s + 32] * (1.0 / math.sqrt(cells // 256))
    for s in range(3):
        detail_ref[s] = second[32 * s : 32 * s + 32] * (1.0 / math.sqrt(cells // 64))
    skip_ref[...] = second[96:] * (1.0 / math.sqrt(cells))
    bias_ref[...] = sum_ref[64:65, :32] * (1.0 / math.sqrt(cells))


def skip_back_kernel(g_ref, skip_ref, out_ref):
    product = dot3(expanded(skip_ref[...], dot), split(tiled(g_ref[...])))
    for t in range(8):
        out_ref[:, 8 * t : 8 * t + 8, :] = product[:, 128 * t : 128 * t + 128].reshape(32, 8, 128)


def unmix_kernel(
    part_ref,
    shares_ref,
    first_ref,
    second_ref,
    coarse_ref,
    detail_ref,
    subband_ref,
    synthesis_ref,
    rows_ref,
    whole,
    scratch,
):
    whole[...] = add_edges(shares_ref, is_even(part_ref), first_ref[...], second_ref[...])
    weights = jnp.concatenate(
        [coarse_ref[s] for s in range(4)] + [detail_ref[s] for s in range(3)], axis=1
    )
    frame = mixed(whole, weights, subband_ref[...], scratch)
    rows_ref[...] = synthesis_rows(frame, lon_synthesis(synthesis_ref))


def field_kernel(part_ref, rows_ref, skip_ref, synthesis_ref, out_ref, field, done):
    lat = lat_filters(synthesis_ref, part_ref)
    stores = []
    for q in range(4):
        part = dot3(lat, split(rows_ref[:, 256 * q : 256 * q + 256]))
        for g in (2 * q, 2 * q + 1):
            channels = slice(4 * g, 4 * g + 4)
            lanes = slice(128 * (g - 2 * q), 128 * (g - 2 * q) + 128)
            field[channels] = skip_ref[channels] + part[:, lanes].reshape(4, 64, 128)
        block = pl.ds(8 * q, 8)
        stores.append(pltpu.make_async_copy(field.at[block], out_ref.at[block], done.at[q]))
        stores[q].start()
    for store in stores:
        store.wait()


def full_spec(shape):
    return pl.BlockSpec(shape, lambda *_: (0,) * len(shape))


def part_spec(shape):
    return pl.BlockSpec(shape, lambda _, part: (part[0] // 2,) + (0,) * (len(shape) - 1))


def shape_of(*shape, dtype=F32):
    return jax.ShapeDtypeStruct(shape, dtype)


FRAME = pltpu.VMEM((512, 128), F32)


def call(kernel, outs, args, part=None, by_part=(), scratch=(), in_hbm=()):
    in_specs = [
        part_spec((1,) + arg.shape[1:]) if i in by_part else full_spec(arg.shape)
        for i, arg in enumerate(args)
    ]
    out_specs = [
        pl.BlockSpec(memory_space=pltpu.HBM) if i in in_hbm else full_spec(out.shape)
        for i, out in enumerate(outs)
    ]
    params = pltpu.CompilerParams(vmem_limit_bytes=48 * 1024 * 1024)
    if part is None:
        return pl.pallas_call(
            kernel,
            grid=(1,),
            in_specs=in_specs,
            out_specs=out_specs,
            out_shape=list(outs),
            scratch_shapes=list(scratch),
            compiler_params=params,
        )(*args)
    grid_spec = pltpu.PrefetchScalarGridSpec(
        num_scalar_prefetch=1,
        grid=(1,),
        in_specs=in_specs,
        out_specs=out_specs,
        scratch_shapes=list(scratch),
    )
    return pl.pallas_call(
        kernel, grid_spec=grid_spec, out_shape=list(outs), compiler_params=params
    )(part, *args)


COEFS = shape_of(512, 128)
ROWS = shape_of(192, 128)
FAR = shape_of(32, 128)
EDGE = shape_of(11, 16, 128)
FIELD = shape_of(32, 64, 128)


def swapped(values, axis, distance):
    count = lax.axis_size(axis)
    return lax.ppermute(values, axis, [(i, i ^ distance) for i in range(count)])


def ring(values, unit):
    count = lax.axis_size("lon")
    step = (3, 1, -1, -3)
    return lax.ppermute(
        values, "lon", [(i, i + step[i // unit % 4] * unit) for i in range(count)]
    )


def middle(values):
    return lax.ppermute(values, "lat", [(1, 2), (2, 1)])


def lat_sum(frame, near, other, far, far_row, part):
    return call(
        functools.partial(lat_sum_kernel, far_row=far_row),
        (COEFS, EDGE, EDGE),
        (jnp.asarray(OWN), frame, near, other, far),
        part,
        (0,),
    )


def lon_exchange(first, second):
    count = lax.axis_size("lon")
    pairs = [(i, (i - 1 + 2 * (i % 2)) % count) for i in range(count)]
    return lax.ppermute(first, "lon", pairs), swapped(second, "lon", 1)


def after(values, others):
    return lax.optimization_barrier((values, others))[0]


def on_device(ocean_field, cotangent, mix_coarse, mix_detail, skip_weight, bias_vector):
    part = (2 * lax.axis_index("lat") + lax.axis_index("lon") % 2).astype(jnp.int32).reshape(1)
    analysis_table, synthesis_table = jnp.asarray(ANALYSIS), jnp.asarray(SYNTHESIS)
    subbands = jnp.asarray(SUBBANDS)
    frame, near, other, far = call(
        analysis_kernel,
        (COEFS, ROWS, ROWS, FAR),
        (ocean_field, analysis_table),
        part,
    )
    (pre,) = call(skip_kernel, (FIELD,), (ocean_field, skip_weight, bias_vector.reshape(1, 32)))
    near = swapped(near, "lat", 1)
    other = middle(other)
    far = swapped(far, "lat", 2)
    (near, other, far), pre = lax.optimization_barrier(((near, other, far), pre))
    shares, first, second = lat_sum(frame, near, other, far, 0, part)
    first, second = lon_exchange(first, second)
    activated, grad_pre, coef, frame, near, other = call(
        forward_kernel,
        (shape_of(32, 64, 128, dtype=BF16), FIELD, COEFS, COEFS, ROWS, ROWS),
        (
            shares,
            first,
            second,
            pre,
            cotangent,
            mix_coarse,
            mix_detail,
            subbands,
            analysis_table,
            synthesis_table,
        ),
        part,
        scratch=(FRAME, pltpu.VMEM((32, 64, 128), BF16), pltpu.SemaphoreType.DMA((4,))),
        in_hbm=(0,),
    )
    (own,) = call(
        weights_kernel,
        (shape_of(264, 128),),
        (ocean_field, grad_pre, coef, frame, near, subbands),
    )
    near = swapped(own, "lat", 1)
    (pair,) = call(pair_kernel, (shape_of(104, 128),), (own, near, frame))
    far = swapped(pair, "lat", 2)
    other = middle(after(other, pair))
    sums = pair[:72] + far[:72]
    steps = [swapped(sums, "lon", k) for k in (4, 12, 8)]
    near, steps[0] = lax.optimization_barrier((near, steps[0]))
    shares, first, second = lat_sum(frame, near, other, far, 72, part)
    grad_pre = after(grad_pre, first)
    (skip_back,) = call(skip_back_kernel, (FIELD,), (grad_pre, skip_weight))
    first, second = lon_exchange(first, second)
    sums = sums + steps[0] + (steps[1] + steps[2])
    steps = [swapped(sums, "lon", k) for k in (16, 48)]
    later, second = lax.optimization_barrier((sums, second))
    steps.append(swapped(later, "lon", 32))
    sums = sums + steps[0] + (steps[1] + steps[2])
    (rows,) = call(
        unmix_kernel,
        (shape_of(256, 1024),),
        (shares, first, second, mix_coarse, mix_detail, subbands, synthesis_table),
        part,
        scratch=(FRAME, FRAME),
    )
    sums, rows = lax.optimization_barrier((sums, rows))
    (grad_field,) = call(
        field_kernel,
        (FIELD,),
        (rows, skip_back, synthesis_table),
        part,
        scratch=(pltpu.VMEM((32, 64, 128), F32), pltpu.SemaphoreType.DMA((4,))),
        in_hbm=(0,),
    )
    steps = [swapped(sums, "lon", k) for k in (1, 3, 2)]
    sums = sums + steps[0] + (steps[1] + steps[2])
    sums, grad_field = lax.optimization_barrier((sums, grad_field))
    cells = LAT_PARTS * LAT_BLOCK * LON_BLOCK * lax.axis_size("lon")
    coarse, detail, grad_skip, grad_bias = call(
        functools.partial(result_kernel, cells=cells),
        (shape_of(4, 32, 32), shape_of(3, 32, 32), shape_of(32, 32), shape_of(1, 32)),
        (sums,),
    )
    return (activated, grad_field, coarse, detail, grad_skip, grad_bias.reshape(32))


def solution(mesh):
    return jax.shard_map(
        on_device,
        mesh=mesh,
        in_specs=(P(None, "lat", "lon"), P(None, "lat", "lon"), P(), P(), P(), P()),
        out_specs=(P(None, "lat", "lon"), P(None, "lat", "lon"), P(), P(), P(), P()),
        check_vma=False,
    )
```

```python
import functools
import math

import jax
import jax.numpy as jnp
import numpy as np
from jax import lax
from jax.experimental import pallas as pl
from jax.experimental.pallas import tpu as pltpu
from jax.sharding import PartitionSpec as P
from ml_dtypes import bfloat16

F32 = jnp.float32
BF16 = jnp.bfloat16

low_taps = (
    -0.010597401785069032,
    0.0328830116668852,
    0.030841381835560764,
    -0.18703481171909309,
    -0.027983769416859854,
    0.6308807679298589,
    0.7148465705529157,
    0.2303778133088965,
)
high_taps = (
    -0.2303778133088965,
    0.7148465705529157,
    -0.6308807679298589,
    -0.027983769416859854,
    0.18703481171909309,
    0.030841381835560764,
    -0.0328830116668852,
    -0.010597401785069032,
)

CHANNELS = 32
LAT_PARTS = 4
LAT_BLOCK = 64
LON_BLOCK = 128
LAT_BAND = (0, 1, 0, 1, 3, 2, 3)
LON_BAND = (0, 0, 1, 1, 2, 3, 3)
LO_LANES = 42
FAR_SHIFT = 32
HI_LANE = 64


def level_matrix(size, taps, periodic):
    matrix = np.zeros((size // 2, size))
    for k in range(size // 2):
        for j in range(8):
            m = 2 * k + j - 3
            if periodic:
                matrix[k, m % size] += taps[j]
            elif 0 <= m < size:
                matrix[k, m] += taps[j]
    return matrix


def composed(size, periodic):
    two = level_matrix(size // 2, low_taps, periodic) @ level_matrix(size, low_taps, periodic)
    three_low = level_matrix(size // 4, low_taps, periodic) @ two
    three_high = level_matrix(size // 4, high_taps, periodic) @ two
    four_low = level_matrix(size // 8, low_taps, periodic) @ three_low
    four_high = level_matrix(size // 8, high_taps, periodic) @ three_low
    return (four_low, four_high, three_low, three_high)


def lane_table():
    lanes = [None] * 128
    coarse_inner, inner = [], []
    for s in range(7):
        count = 14 if s < 4 else 22
        for e in range(6):
            lanes[s * 6 + e] = (s, e)
            lanes[HI_LANE + s * 6 + e] = (s, count - 6 + e)
        target = coarse_inner if s < 4 else inner
        target += [(s, e) for e in range(6, count - 6)]
    lanes[HI_LANE - 8 : HI_LANE] = coarse_inner
    free = [lane for lane in range(128) if lanes[lane] is None]
    for lane, entry in zip(free, inner):
        lanes[lane] = entry
    return lanes


LANES = lane_table()
SUBBAND_OF_LANE = np.array([-1 if entry is None else entry[0] for entry in LANES])


def lon_weights():
    maps = composed(8 * LON_BLOCK, True)
    start = 3 * LON_BLOCK
    weights = np.zeros((4, LON_BLOCK, 128))
    for lane, entry in enumerate(LANES):
        if entry is None:
            continue
        s, e = entry
        per_block = 8 if s < 4 else 16
        row = maps[LON_BAND[s]][3 * per_block - 3 + e]
        weights[LAT_BAND[s], :, lane] = row[start : start + LON_BLOCK]
    return weights.reshape(4 * LON_BLOCK, 128)


def row_entries(part):
    top4, bottom4 = list(range(6)) + [None] * 2, list(range(4, 10)) + [None] * 2
    top3, bottom3 = list(range(8)), list(range(8, 14)) + [None] * 2
    four = bottom4 + top4 if part % 2 == 0 else top4 + bottom4
    three = bottom3 + top3 if part % 2 == 0 else top3 + bottom3
    four[14:16] = [8, 9] if part < 2 else [0, 1]
    return four, three


def lat_weights():
    maps = composed(LAT_PARTS * LAT_BLOCK, False)
    weights = np.zeros((LAT_PARTS, 4, 16, LAT_BLOCK))
    for part in range(LAT_PARTS):
        entries = row_entries(part)
        for band in range(4):
            per_block = 4 if band < 2 else 8
            for row, e in enumerate(entries[0 if band < 2 else 1]):
                k = per_block * part - 3 + e if e is not None else -1
                if 0 <= k < per_block * LAT_PARTS:
                    weights[part, band, row] = maps[band][
                        k, part * LAT_BLOCK : (part + 1) * LAT_BLOCK
                    ]
    return weights.reshape(LAT_PARTS, 64, LAT_BLOCK)


def own_mask():
    mask = np.ones((LAT_PARTS, 16, 128), np.float32)
    four = (SUBBAND_OF_LANE >= 0) & (SUBBAND_OF_LANE < 4)
    for part in range(LAT_PARTS):
        bottom = 0 if part % 2 == 0 else 8
        for row in (bottom, bottom + 1, 14, 15):
            mask[part, row, four] = 0.0
    return mask


def high_low(matrix):
    matrix = matrix.astype(np.float32)
    high = matrix.astype(bfloat16)
    low = (matrix - high.astype(np.float32)).astype(bfloat16)
    return np.stack([high, low], axis=-3)


LON = lon_weights()
LAT = lat_weights()
LON_ROWS = 1024


def packed(lon, lat):
    lon = high_low(lon)
    lon = np.concatenate(
        [lon[:, :, 128 * b : 128 * b + 128] for b in range(lon.shape[2] // 128)], axis=1
    )
    lat = high_low(np.tile(lat, (1, 1, 2)))
    return np.concatenate([lon.reshape(LON_ROWS, 128), lat.reshape(-1, 128)])


ANALYSIS = packed(LON, LAT)
SYNTHESIS = packed(LON.T, LAT.transpose(0, 2, 1))
OWN = own_mask()
SUBBANDS = np.tile(SUBBAND_OF_LANE.astype(np.float32), (8, 1))


def split(x):
    high = x.astype(BF16)
    low = (x - high.astype(F32)).astype(BF16)
    return high, low


def dot(a, b):
    return jnp.dot(a, b, preferred_element_type=F32)


def dot_nt(a, b):
    return lax.dot_general(a, b, (((1,), (1,)), ((), ())), preferred_element_type=F32)


def dot3(a, b, product=dot):
    return product(a[0], b[0]) + (product(a[0], b[1]) + product(a[1], b[0]))


def lat_matrix(block):
    row = lax.broadcasted_iota(jnp.int32, (256, 256), 0)
    keep = row // 64 == lane_index((256, 256)) // 64
    return tuple(
        jnp.where(keep, jnp.tile(block[64 * k : 64 * k + 64], (4, 2)), 0.0).astype(BF16)
        for k in range(2)
    )


def lat_filters(table_ref, part_ref):
    first = pl.multiple_of(LON_ROWS + 128 * lat_part(part_ref), 128)
    return lat_matrix(table_ref[pl.ds(first, 128), :])


def lon_analysis(table_ref):
    return table_ref[0:512], table_ref[512:1024]


def lon_synthesis(table_ref):
    return tuple(
        jnp.concatenate(
            [table_ref[512 * k + 128 * b : 512 * k + 128 * b + 128] for b in range(4)], axis=1
        )
        for k in range(2)
    )


def lat_part(part_ref):
    return part_ref[0] // 2


def is_even(part_ref):
    return part_ref[0] % 2 == 0


def grouped(x):
    return jnp.concatenate(
        [x[4 * g : 4 * g + 4].reshape(256, 128) for g in range(x.shape[0] // 4)], axis=1
    )


def tiled(x):
    return jnp.concatenate(
        [x[:, 8 * t : 8 * t + 8, :].reshape(256, 128) for t in range(8)], axis=1
    )


def analysis(groups, lat, lon):
    rows = dot3(lat, split(groups))
    count = groups.shape[1] // 128
    blocks = []
    for g in range(count):
        part = rows[:, 128 * g : 128 * g + 128].reshape(4, 4, 16, 128)
        blocks.append(
            jnp.concatenate([part[:, b].reshape(64, 128) for b in range(4)], axis=1)
        )
    return dot3(split(jnp.concatenate(blocks, axis=0)), lon).reshape(4 * count, 16, 128)


def synthesis_rows(frame, lon):
    wide = dot3(split(frame), lon).reshape(-1, 4, 16, 512)
    groups = []
    for g in range(wide.shape[0]):
        part = jnp.stack(
            [wide[g, :, :, 128 * b : 128 * b + 128] for b in range(4)], axis=1
        )
        groups.append(part.reshape(256, 128))
    return jnp.concatenate(groups, axis=1)


def lane_index(shape):
    return lax.broadcasted_iota(jnp.int32, shape, len(shape) - 1)


def rolled(x, shift):
    return pltpu.roll(x, shift % 128, 2) if shift % 128 else x


def edge_lanes(frame, first):
    lane = lane_index((11, 16, 128))
    parts = [rolled(frame[c : c + 11], LO_LANES * k - first) for k, c in enumerate((0, 11, 21))]
    return jnp.where(
        lane < LO_LANES, parts[0], jnp.where(lane < 2 * LO_LANES, parts[1], parts[2])
    )


def placed_lanes(edge, first):
    parts = [rolled(edge, first - LO_LANES * k) for k in range(3)]
    whole = jnp.concatenate([parts[0], parts[1], parts[2][1:]], axis=0)
    lane = lane_index(whole.shape)
    return jnp.where((lane >= first) & (lane < first + LO_LANES), whole, 0.0)


def add_edges(frame_ref, even, first, second):
    from_left = jnp.where(even, first, second)
    from_right = jnp.where(even, second, first)
    added = placed_lanes(from_left, 0) + placed_lanes(from_right, HI_LANE)
    return frame_ref[...] + added.reshape(512, 128)


def by_row(frame_ref):
    return jnp.concatenate([frame_ref[pl.ds(r, 32, stride=16), :] for r in range(16)], axis=1)


def stacked(data, subbands):
    masks = [
        jnp.concatenate([(subbands[0:1] == float(s)).astype(BF16)] * 16, axis=1) for s in range(7)
    ]
    return [jnp.concatenate([part * mask for mask in masks], axis=0) for part in split(data)]


def mixed(frame_ref, weights, subbands, scratch):
    data = stacked(by_row(frame_ref), subbands)
    high, low = split(weights)
    double = dot(jnp.concatenate([high, low], axis=0), data[0])
    result = double[:32] + (double[32:] + dot(high, data[1]))
    for r in range(16):
        scratch[pl.ds(r, 32, stride=16), :] = result[:, 128 * r : 128 * r + 128]
    return scratch[...]


def coarse_lanes():
    lane = lane_index((1, 128))
    return (lane < 24) | ((lane >= HI_LANE - 8) & (lane < HI_LANE + 24))


def store_frame(frame, frame_ref, near_ref, other_ref):
    frame_ref[...] = frame.reshape(512, 128)
    for target, first in ((near_ref, 0), (other_ref, 8)):
        for r in range(6):
            target[32 * r : 32 * r + 32] = frame_ref[pl.ds(first + r, 32, stride=16), :]


def far_rows(frame_ref):
    coarse = coarse_lanes()
    rows = [jnp.where(coarse, frame_ref[pl.ds(14 + r, 32, stride=16), :], 0.0) for r in range(2)]
    return rows[0] + pltpu.roll(rows[1], FAR_SHIFT, 1)


def analysis_kernel(part_ref, x_ref, table_ref, frame_ref, near_ref, other_ref, far_ref):
    lat = lat_filters(table_ref, part_ref)
    frame = analysis(grouped(x_ref[...]), lat, lon_analysis(table_ref))
    store_frame(frame, frame_ref, near_ref, other_ref)
    far_ref[...] = far_rows(frame_ref)


def expand_matrix():
    row = lax.broadcasted_iota(jnp.int32, (256, 32), 0)
    return (row // 8 == lane_index((256, 32))).astype(BF16)


def same_row(shape):
    row = lax.broadcasted_iota(jnp.int32, shape, 0)
    return lax.rem(row, 8) == lax.rem(lane_index(shape), 8)


def expanded(weight, product):
    expand = expand_matrix()
    diagonal = same_row((256, 256))
    return tuple(
        jnp.where(diagonal, dot_nt(product(expand, part).astype(BF16), expand), 0.0).astype(BF16)
        for part in split(weight)
    )


def skip_kernel(x_ref, skip_ref, bias_ref, pre_ref):
    weight = expanded(skip_ref[...], dot_nt)
    product = dot3(weight, split(tiled(x_ref[...])))
    bias = jnp.sum(expand_matrix().astype(F32) * bias_ref[...], axis=1, keepdims=True)
    for t in range(8):
        pre_ref[:, 8 * t : 8 * t + 8, :] = (
            product[:, 128 * t : 128 * t + 128] + bias
        ).reshape(32, 8, 128)


def lat_sum_kernel(
    part_ref,
    mask_ref,
    frame_ref,
    near_ref,
    other_ref,
    far_ref,
    sum_ref,
    first_ref,
    second_ref,
    *,
    far_row,
):
    frame = frame_ref[...].reshape(32, 16, 128) * mask_ref[0][None]
    sum_ref[...] = frame.reshape(512, 128)
    coarse = coarse_lanes()
    for r in range(6):
        sum_ref[pl.ds(r, 32, stride=16), :] += near_ref[32 * r : 32 * r + 32]
        sum_ref[pl.ds(8 + r, 32, stride=16), :] += other_ref[32 * r : 32 * r + 32]
    far = far_ref[far_row : far_row + 32]
    for r, shared in enumerate((far, pltpu.roll(far, 128 - FAR_SHIFT, 1))):
        sum_ref[pl.ds(14 + r, 32, stride=16), :] += jnp.where(coarse, shared, 0.0)
    frame = sum_ref[...].reshape(32, 16, 128)
    low, high = edge_lanes(frame, 0), edge_lanes(frame, HI_LANE)
    even = is_even(part_ref)
    first_ref[...] = jnp.where(even, low, high)
    second_ref[...] = jnp.where(even, high, low)


def forward_kernel(
    part_ref,
    shares_ref,
    first_ref,
    second_ref,
    pre_ref,
    cot_ref,
    coarse_ref,
    detail_ref,
    subband_ref,
    analysis_ref,
    synthesis_ref,
    act_ref,
    grad_ref,
    coef_ref,
    frame_ref,
    near_ref,
    other_ref,
    scratch,
    act,
    done,
):
    coef_ref[...] = add_edges(
        shares_ref, is_even(part_ref), first_ref[...], second_ref[...]
    )
    weights = jnp.concatenate(
        [coarse_ref[s].T for s in range(4)] + [detail_ref[s].T for s in range(3)], axis=1
    )
    frame = mixed(coef_ref, weights, subband_ref[...], scratch)
    lon = lon_synthesis(synthesis_ref)
    lat = lat_filters(synthesis_ref, part_ref)
    grads = []
    stores = []
    for q in range(4):
        kernel = dot3(lat, split(synthesis_rows(frame[128 * q : 128 * q + 128], lon)))
        for g in (2 * q, 2 * q + 1):
            channels = slice(4 * g, 4 * g + 4)
            lanes = slice(128 * (g - 2 * q), 128 * (g - 2 * q) + 128)
            pre = kernel[:, lanes] + pre_ref[channels].reshape(256, 128)
            cumulative = 0.5 * (1.0 + lax.erf(pre * math.sqrt(0.5)))
            density = jnp.exp(-0.5 * pre * pre) * (1.0 / math.sqrt(2.0 * math.pi))
            act[channels] = (pre * cumulative).astype(BF16).reshape(4, 64, 128)
            grad = cot_ref[channels].astype(F32).reshape(256, 128) * (cumulative + pre * density)
            grad_ref[channels] = grad.reshape(4, 64, 128)
            grads.append(grad)
        block = pl.ds(8 * q, 8)
        stores.append(pltpu.make_async_copy(act.at[block], act_ref.at[block], done.at[q]))
        stores[q].start()
    frame = analysis(
        jnp.concatenate(grads, axis=1),
        lat_filters(analysis_ref, part_ref),
        lon_analysis(analysis_ref),
    )
    store_frame(frame, frame_ref, near_ref, other_ref)
    for store in stores:
        store.wait()


def weights_kernel(x_ref, g_ref, coef_ref, frame_ref, near_ref, subband_ref, sum_ref):
    def placed(parts, offset):
        row = lax.broadcasted_iota(jnp.int32, (256, 128), 0)
        place = (row // 8 + offset == lane_index((256, 128))).astype(BF16)
        return dot(parts[0], place) + dot(parts[1], place)

    coef = stacked(by_row(coef_ref), subband_ref[...])
    high, low = split(by_row(frame_ref))
    double = dot_nt(jnp.concatenate([high, low], axis=0), coef[0])
    mix = double[:32] + (double[32:] + dot_nt(high, coef[1]))
    mix = jnp.concatenate([mix, jnp.zeros((32, 32), F32)], axis=1)
    field = split(tiled(x_ref[...]))
    grad_pre = split(tiled(g_ref[...]))
    product = jnp.where(same_row((256, 256)), dot3(grad_pre, field, dot_nt), 0.0)
    skip = split(jnp.sum(product.reshape(32, 8, 256), axis=1))
    rows = split(jnp.sum(g_ref[...].reshape(32, 8, 8, 128), axis=1).reshape(256, 128))
    ones = jnp.ones((8, 128), BF16)
    bias = split(dot_nt(ones, rows[0]) + dot_nt(ones, rows[1]))
    sum_ref[0:192] = near_ref[...]
    sum_ref[192:224] = mix[:, :128]
    sum_ref[224:256] = mix[:, 128:] + placed(skip, 96)
    sum_ref[256:264] = placed(bias, 0)


def pair_kernel(own_ref, near_ref, frame_ref, out_ref):
    out_ref[0:72] = own_ref[192:264] + near_ref[192:264]
    out_ref[72:104] = far_rows(frame_ref)


def result_kernel(sum_ref, coarse_ref, detail_ref, skip_ref, bias_ref, cells):
    first = sum_ref[0:32].T
    second = sum_ref[32:64].T
    for s in range(4):
        coarse_ref[s] = first[32 * s : 32 * s + 32] * (1.0 / math.sqrt(cells // 256))
    for s in range(3):
        detail_ref[s] = second[32 * s : 32 * s + 32] * (1.0 / math.sqrt(cells // 64))
    skip_ref[...] = second[96:] * (1.0 / math.sqrt(cells))
    bias_ref[...] = sum_ref[64:65, :32] * (1.0 / math.sqrt(cells))


def skip_back_kernel(g_ref, skip_ref, out_ref):
    product = dot3(expanded(skip_ref[...], dot), split(tiled(g_ref[...])))
    for t in range(8):
        out_ref[:, 8 * t : 8 * t + 8, :] = product[:, 128 * t : 128 * t + 128].reshape(32, 8, 128)


def unmix_kernel(
    part_ref,
    shares_ref,
    first_ref,
    second_ref,
    coarse_ref,
    detail_ref,
    subband_ref,
    synthesis_ref,
    rows_ref,
    whole,
    scratch,
):
    whole[...] = add_edges(shares_ref, is_even(part_ref), first_ref[...], second_ref[...])
    weights = jnp.concatenate(
        [coarse_ref[s] for s in range(4)] + [detail_ref[s] for s in range(3)], axis=1
    )
    frame = mixed(whole, weights, subband_ref[...], scratch)
    rows_ref[...] = synthesis_rows(frame, lon_synthesis(synthesis_ref))


def field_kernel(part_ref, rows_ref, skip_ref, synthesis_ref, out_ref, field, done):
    lat = lat_filters(synthesis_ref, part_ref)
    stores = []
    for q in range(4):
        part = dot3(lat, split(rows_ref[:, 256 * q : 256 * q + 256]))
        for g in (2 * q, 2 * q + 1):
            channels = slice(4 * g, 4 * g + 4)
            lanes = slice(128 * (g - 2 * q), 128 * (g - 2 * q) + 128)
            field[channels] = skip_ref[channels] + part[:, lanes].reshape(4, 64, 128)
        block = pl.ds(8 * q, 8)
        stores.append(pltpu.make_async_copy(field.at[block], out_ref.at[block], done.at[q]))
        stores[q].start()
    for store in stores:
        store.wait()


def full_spec(shape):
    return pl.BlockSpec(shape, lambda *_: (0,) * len(shape))


def part_spec(shape):
    return pl.BlockSpec(shape, lambda _, part: (part[0] // 2,) + (0,) * (len(shape) - 1))


def shape_of(*shape, dtype=F32):
    return jax.ShapeDtypeStruct(shape, dtype)


FRAME = pltpu.VMEM((512, 128), F32)


def call(kernel, outs, args, part=None, by_part=(), scratch=(), in_hbm=()):
    in_specs = [
        part_spec((1,) + arg.shape[1:]) if i in by_part else full_spec(arg.shape)
        for i, arg in enumerate(args)
    ]
    out_specs = [
        pl.BlockSpec(memory_space=pltpu.HBM) if i in in_hbm else full_spec(out.shape)
        for i, out in enumerate(outs)
    ]
    params = pltpu.CompilerParams(vmem_limit_bytes=48 * 1024 * 1024)
    if part is None:
        return pl.pallas_call(
            kernel,
            grid=(1,),
            in_specs=in_specs,
            out_specs=out_specs,
            out_shape=list(outs),
            scratch_shapes=list(scratch),
            compiler_params=params,
        )(*args)
    grid_spec = pltpu.PrefetchScalarGridSpec(
        num_scalar_prefetch=1,
        grid=(1,),
        in_specs=in_specs,
        out_specs=out_specs,
        scratch_shapes=list(scratch),
    )
    return pl.pallas_call(
        kernel, grid_spec=grid_spec, out_shape=list(outs), compiler_params=params
    )(part, *args)


COEFS = shape_of(512, 128)
ROWS = shape_of(192, 128)
FAR = shape_of(32, 128)
EDGE = shape_of(11, 16, 128)
FIELD = shape_of(32, 64, 128)


def swapped(values, axis, distance):
    count = lax.axis_size(axis)
    return lax.ppermute(values, axis, [(i, i ^ distance) for i in range(count)])


def ring(values, unit):
    count = lax.axis_size("lon")
    step = (3, 1, -1, -3)
    return lax.ppermute(
        values, "lon", [(i, i + step[i // unit % 4] * unit) for i in range(count)]
    )


def across(values):
    pairs = []
    for lon in range(lax.axis_size("lon")):
        for lat in range(LAT_PARTS):
            other = lat ^ 2 if lon % 4 in (0, 3) else lat
            pairs.append((LAT_PARTS * lon + lat, LAT_PARTS * (lon ^ 3) + other))
    return lax.ppermute(values, ("lon", "lat"), pairs)


def middle(values):
    return lax.ppermute(values, "lat", [(1, 2), (2, 1)])


def lat_sum(frame, near, other, far, far_row, part):
    return call(
        functools.partial(lat_sum_kernel, far_row=far_row),
        (COEFS, EDGE, EDGE),
        (jnp.asarray(OWN), frame, near, other, far),
        part,
        (0,),
    )


def lon_exchange(first, second):
    count = lax.axis_size("lon")
    pairs = [(i, (i - 1 + 2 * (i % 2)) % count) for i in range(count)]
    return lax.ppermute(first, "lon", pairs), swapped(second, "lon", 1)


def after(values, others):
    return lax.optimization_barrier((values, others))[0]


def on_device(ocean_field, cotangent, mix_coarse, mix_detail, skip_weight, bias_vector):
    part = (2 * lax.axis_index("lat") + lax.axis_index("lon") % 2).astype(jnp.int32).reshape(1)
    analysis_table, synthesis_table = jnp.asarray(ANALYSIS), jnp.asarray(SYNTHESIS)
    subbands = jnp.asarray(SUBBANDS)
    frame, near, other, far = call(
        analysis_kernel,
        (COEFS, ROWS, ROWS, FAR),
        (ocean_field, analysis_table),
        part,
    )
    (pre,) = call(skip_kernel, (FIELD,), (ocean_field, skip_weight, bias_vector.reshape(1, 32)))
    near = swapped(near, "lat", 1)
    other = middle(other)
    far = swapped(far, "lat", 2)
    (near, other, far), pre = lax.optimization_barrier(((near, other, far), pre))
    shares, first, second = lat_sum(frame, near, other, far, 0, part)
    first, second = lon_exchange(first, second)
    activated, grad_pre, coef, frame, near, other = call(
        forward_kernel,
        (shape_of(32, 64, 128, dtype=BF16), FIELD, COEFS, COEFS, ROWS, ROWS),
        (
            shares,
            first,
            second,
            pre,
            cotangent,
            mix_coarse,
            mix_detail,
            subbands,
            analysis_table,
            synthesis_table,
        ),
        part,
        scratch=(FRAME, pltpu.VMEM((32, 64, 128), BF16), pltpu.SemaphoreType.DMA((4,))),
        in_hbm=(0,),
    )
    (own,) = call(
        weights_kernel,
        (shape_of(264, 128),),
        (ocean_field, grad_pre, coef, frame, near, subbands),
    )
    (skip_back,) = call(skip_back_kernel, (FIELD,), (grad_pre, skip_weight))
    near = swapped(own, "lat", 1)
    near, skip_back = lax.optimization_barrier((near, skip_back))
    (pair,) = call(pair_kernel, (shape_of(104, 128),), (own, near, frame))
    far = swapped(pair, "lat", 2)
    other = middle(after(other, pair))
    sums = pair[:72] + far[:72]
    steps = [swapped(sums, "lon", k) for k in (4, 12, 8)]
    shares, first, second = lat_sum(frame, near, other, far, 72, part)
    first, second = lon_exchange(first, second)
    sums = sums + steps[0] + (steps[1] + steps[2])
    steps = [swapped(sums, "lon", k) for k in (16, 48)]
    later, second = lax.optimization_barrier((sums, second))
    steps.append(swapped(later, "lon", 32))
    sums = sums + steps[0] + (steps[1] + steps[2])
    (rows,) = call(
        unmix_kernel,
        (shape_of(256, 1024),),
        (shares, first, second, mix_coarse, mix_detail, subbands, synthesis_table),
        part,
        scratch=(FRAME, FRAME),
    )
    sums, rows = lax.optimization_barrier((sums, rows))
    (grad_field,) = call(
        field_kernel,
        (FIELD,),
        (rows, skip_back, synthesis_table),
        part,
        scratch=(pltpu.VMEM((32, 64, 128), F32), pltpu.SemaphoreType.DMA((4,))),
        in_hbm=(0,),
    )
    steps = [swapped(sums, "lon", 1), across(sums), swapped(sums, "lon", 2)]
    sums = sums + steps[0] + (steps[1] + steps[2])
    sums, grad_field = lax.optimization_barrier((sums, grad_field))
    cells = LAT_PARTS * LAT_BLOCK * LON_BLOCK * lax.axis_size("lon")
    coarse, detail, grad_skip, grad_bias = call(
        functools.partial(result_kernel, cells=cells),
        (shape_of(4, 32, 32), shape_of(3, 32, 32), shape_of(32, 32), shape_of(1, 32)),
        (sums,),
    )
    return (activated, grad_field, coarse, detail, grad_skip, grad_bias.reshape(32))


def solution(mesh):
    return jax.shard_map(
        on_device,
        mesh=mesh,
        in_specs=(P(None, "lat", "lon"), P(None, "lat", "lon"), P(), P(), P(), P()),
        out_specs=(P(None, "lat", "lon"), P(None, "lat", "lon"), P(), P(), P(), P()),
        check_vma=False,
    )
```

```python
import functools
import math

import jax
import jax.numpy as jnp
import numpy as np
from jax import lax
from jax.experimental import pallas as pl
from jax.experimental.pallas import tpu as pltpu
from jax.sharding import PartitionSpec as P
from ml_dtypes import bfloat16

F32 = jnp.float32
BF16 = jnp.bfloat16

low_taps = (
    -0.010597401785069032,
    0.0328830116668852,
    0.030841381835560764,
    -0.18703481171909309,
    -0.027983769416859854,
    0.6308807679298589,
    0.7148465705529157,
    0.2303778133088965,
)
high_taps = (
    -0.2303778133088965,
    0.7148465705529157,
    -0.6308807679298589,
    -0.027983769416859854,
    0.18703481171909309,
    0.030841381835560764,
    -0.0328830116668852,
    -0.010597401785069032,
)

CHANNELS = 32
LAT_PARTS = 4
LAT_BLOCK = 64
LON_BLOCK = 128
LAT_BAND = (0, 1, 0, 1, 3, 2, 3)
LON_BAND = (0, 0, 1, 1, 2, 3, 3)
LO_LANES = 42
FAR_SHIFT = 32
HI_LANE = 64


def level_matrix(size, taps, periodic):
    matrix = np.zeros((size // 2, size))
    for k in range(size // 2):
        for j in range(8):
            m = 2 * k + j - 3
            if periodic:
                matrix[k, m % size] += taps[j]
            elif 0 <= m < size:
                matrix[k, m] += taps[j]
    return matrix


def composed(size, periodic):
    two = level_matrix(size // 2, low_taps, periodic) @ level_matrix(size, low_taps, periodic)
    three_low = level_matrix(size // 4, low_taps, periodic) @ two
    three_high = level_matrix(size // 4, high_taps, periodic) @ two
    four_low = level_matrix(size // 8, low_taps, periodic) @ three_low
    four_high = level_matrix(size // 8, high_taps, periodic) @ three_low
    return (four_low, four_high, three_low, three_high)


def lane_table():
    lanes = [None] * 128
    coarse_inner, inner = [], []
    for s in range(7):
        count = 14 if s < 4 else 22
        for e in range(6):
            lanes[s * 6 + e] = (s, e)
            lanes[HI_LANE + s * 6 + e] = (s, count - 6 + e)
        target = coarse_inner if s < 4 else inner
        target += [(s, e) for e in range(6, count - 6)]
    lanes[HI_LANE - 8 : HI_LANE] = coarse_inner
    free = [lane for lane in range(128) if lanes[lane] is None]
    for lane, entry in zip(free, inner):
        lanes[lane] = entry
    return lanes


LANES = lane_table()
SUBBAND_OF_LANE = np.array([-1 if entry is None else entry[0] for entry in LANES])


def lon_weights():
    maps = composed(8 * LON_BLOCK, True)
    start = 3 * LON_BLOCK
    weights = np.zeros((4, LON_BLOCK, 128))
    for lane, entry in enumerate(LANES):
        if entry is None:
            continue
        s, e = entry
        per_block = 8 if s < 4 else 16
        row = maps[LON_BAND[s]][3 * per_block - 3 + e]
        weights[LAT_BAND[s], :, lane] = row[start : start + LON_BLOCK]
    return weights.reshape(4 * LON_BLOCK, 128)


def row_entries(part):
    top4, bottom4 = list(range(6)) + [None] * 2, list(range(4, 10)) + [None] * 2
    top3, bottom3 = list(range(8)), list(range(8, 14)) + [None] * 2
    four = bottom4 + top4 if part % 2 == 0 else top4 + bottom4
    three = bottom3 + top3 if part % 2 == 0 else top3 + bottom3
    four[14:16] = [8, 9] if part < 2 else [0, 1]
    return four, three


def lat_weights():
    maps = composed(LAT_PARTS * LAT_BLOCK, False)
    weights = np.zeros((LAT_PARTS, 4, 16, LAT_BLOCK))
    for part in range(LAT_PARTS):
        entries = row_entries(part)
        for band in range(4):
            per_block = 4 if band < 2 else 8
            for row, e in enumerate(entries[0 if band < 2 else 1]):
                k = per_block * part - 3 + e if e is not None else -1
                if 0 <= k < per_block * LAT_PARTS:
                    weights[part, band, row] = maps[band][
                        k, part * LAT_BLOCK : (part + 1) * LAT_BLOCK
                    ]
    return weights.reshape(LAT_PARTS, 64, LAT_BLOCK)


def own_mask():
    mask = np.ones((LAT_PARTS, 16, 128), np.float32)
    four = (SUBBAND_OF_LANE >= 0) & (SUBBAND_OF_LANE < 4)
    for part in range(LAT_PARTS):
        bottom = 0 if part % 2 == 0 else 8
        for row in (bottom, bottom + 1, 14, 15):
            mask[part, row, four] = 0.0
    return mask


def high_low(matrix):
    matrix = matrix.astype(np.float32)
    high = matrix.astype(bfloat16)
    low = (matrix - high.astype(np.float32)).astype(bfloat16)
    return np.stack([high, low], axis=-3)


LON = lon_weights()
LAT = lat_weights()
LON_ROWS = 1024


def packed(lon, lat):
    lon = high_low(lon)
    lon = np.concatenate(
        [lon[:, :, 128 * b : 128 * b + 128] for b in range(lon.shape[2] // 128)], axis=1
    )
    lat = high_low(np.tile(lat, (1, 1, 2)))
    return np.concatenate([lon.reshape(LON_ROWS, 128), lat.reshape(-1, 128)])


ANALYSIS = packed(LON, LAT)
SYNTHESIS = packed(LON.T, LAT.transpose(0, 2, 1))
OWN = own_mask()
SUBBANDS = np.tile(SUBBAND_OF_LANE.astype(np.float32), (8, 1))


def split(x):
    high = x.astype(BF16)
    low = (x - high.astype(F32)).astype(BF16)
    return high, low


def dot(a, b):
    return jnp.dot(a, b, preferred_element_type=F32)


def dot_nt(a, b):
    return lax.dot_general(a, b, (((1,), (1,)), ((), ())), preferred_element_type=F32)


def dot3(a, b, product=dot):
    return product(a[0], b[0]) + (product(a[0], b[1]) + product(a[1], b[0]))


def lat_matrix(block):
    row = lax.broadcasted_iota(jnp.int32, (256, 256), 0)
    keep = row // 64 == lane_index((256, 256)) // 64
    return tuple(
        jnp.where(keep, jnp.tile(block[64 * k : 64 * k + 64], (4, 2)), 0.0).astype(BF16)
        for k in range(2)
    )


def lat_filters(table_ref, part_ref):
    first = pl.multiple_of(LON_ROWS + 128 * lat_part(part_ref), 128)
    return lat_matrix(table_ref[pl.ds(first, 128), :])


def lon_analysis(table_ref):
    return table_ref[0:512], table_ref[512:1024]


def lon_synthesis(table_ref):
    return tuple(
        jnp.concatenate(
            [table_ref[512 * k + 128 * b : 512 * k + 128 * b + 128] for b in range(4)], axis=1
        )
        for k in range(2)
    )


def lat_part(part_ref):
    return part_ref[0] // 2


def is_even(part_ref):
    return part_ref[0] % 2 == 0


def grouped(x):
    return jnp.concatenate(
        [x[4 * g : 4 * g + 4].reshape(256, 128) for g in range(x.shape[0] // 4)], axis=1
    )


def tiled(x):
    return jnp.concatenate(
        [x[:, 8 * t : 8 * t + 8, :].reshape(256, 128) for t in range(8)], axis=1
    )


def analysis(groups, lat, lon):
    rows = dot3(lat, split(groups))
    count = groups.shape[1] // 128
    blocks = []
    for g in range(count):
        part = rows[:, 128 * g : 128 * g + 128].reshape(4, 4, 16, 128)
        blocks.append(
            jnp.concatenate([part[:, b].reshape(64, 128) for b in range(4)], axis=1)
        )
    return dot3(split(jnp.concatenate(blocks, axis=0)), lon).reshape(4 * count, 16, 128)


def synthesis_rows(frame, lon):
    wide = dot3(split(frame), lon).reshape(-1, 4, 16, 512)
    groups = []
    for g in range(wide.shape[0]):
        part = jnp.stack(
            [wide[g, :, :, 128 * b : 128 * b + 128] for b in range(4)], axis=1
        )
        groups.append(part.reshape(256, 128))
    return jnp.concatenate(groups, axis=1)


def lane_index(shape):
    return lax.broadcasted_iota(jnp.int32, shape, len(shape) - 1)


def rolled(x, shift):
    return pltpu.roll(x, shift % 128, 2) if shift % 128 else x


def edge_lanes(frame, first):
    lane = lane_index((11, 16, 128))
    parts = [rolled(frame[c : c + 11], LO_LANES * k - first) for k, c in enumerate((0, 11, 21))]
    return jnp.where(
        lane < LO_LANES, parts[0], jnp.where(lane < 2 * LO_LANES, parts[1], parts[2])
    )


def placed_lanes(edge, first):
    parts = [rolled(edge, first - LO_LANES * k) for k in range(3)]
    whole = jnp.concatenate([parts[0], parts[1], parts[2][1:]], axis=0)
    lane = lane_index(whole.shape)
    return jnp.where((lane >= first) & (lane < first + LO_LANES), whole, 0.0)


def add_edges(frame_ref, even, first, second):
    from_left = jnp.where(even, first, second)
    from_right = jnp.where(even, second, first)
    added = placed_lanes(from_left, 0) + placed_lanes(from_right, HI_LANE)
    return frame_ref[...] + added.reshape(512, 128)


def by_row(frame_ref):
    return jnp.concatenate([frame_ref[pl.ds(r, 32, stride=16), :] for r in range(16)], axis=1)


def stacked(data, subbands):
    masks = [
        jnp.concatenate([(subbands[0:1] == float(s)).astype(BF16)] * 16, axis=1) for s in range(7)
    ]
    return [jnp.concatenate([part * mask for mask in masks], axis=0) for part in split(data)]


def mixed(frame_ref, weights, subbands, scratch):
    data = stacked(by_row(frame_ref), subbands)
    high, low = split(weights)
    double = dot(jnp.concatenate([high, low], axis=0), data[0])
    result = double[:32] + (double[32:] + dot(high, data[1]))
    for r in range(16):
        scratch[pl.ds(r, 32, stride=16), :] = result[:, 128 * r : 128 * r + 128]
    return scratch[...]


def coarse_lanes():
    lane = lane_index((1, 128))
    return (lane < 24) | ((lane >= HI_LANE - 8) & (lane < HI_LANE + 24))


def store_frame(frame, frame_ref, near_ref, other_ref):
    frame_ref[...] = frame.reshape(512, 128)
    for target, first in ((near_ref, 0), (other_ref, 8)):
        for r in range(6):
            target[32 * r : 32 * r + 32] = frame_ref[pl.ds(first + r, 32, stride=16), :]


def far_rows(frame_ref):
    coarse = coarse_lanes()
    rows = [jnp.where(coarse, frame_ref[pl.ds(14 + r, 32, stride=16), :], 0.0) for r in range(2)]
    return rows[0] + pltpu.roll(rows[1], FAR_SHIFT, 1)


def analysis_kernel(part_ref, x_ref, table_ref, frame_ref, near_ref, other_ref, far_ref):
    lat = lat_filters(table_ref, part_ref)
    frame = analysis(grouped(x_ref[...]), lat, lon_analysis(table_ref))
    store_frame(frame, frame_ref, near_ref, other_ref)
    far_ref[...] = far_rows(frame_ref)


def expand_matrix():
    row = lax.broadcasted_iota(jnp.int32, (256, 32), 0)
    return (row // 8 == lane_index((256, 32))).astype(BF16)


def same_row(shape):
    row = lax.broadcasted_iota(jnp.int32, shape, 0)
    return lax.rem(row, 8) == lax.rem(lane_index(shape), 8)


def expanded(weight, product):
    expand = expand_matrix()
    diagonal = same_row((256, 256))
    return tuple(
        jnp.where(diagonal, dot_nt(product(expand, part).astype(BF16), expand), 0.0).astype(BF16)
        for part in split(weight)
    )


def skip_kernel(x_ref, skip_ref, bias_ref, pre_ref):
    weight = expanded(skip_ref[...], dot_nt)
    product = dot3(weight, split(tiled(x_ref[...])))
    bias = jnp.sum(expand_matrix().astype(F32) * bias_ref[...], axis=1, keepdims=True)
    for t in range(8):
        pre_ref[:, 8 * t : 8 * t + 8, :] = (
            product[:, 128 * t : 128 * t + 128] + bias
        ).reshape(32, 8, 128)


def lat_sum_kernel(
    part_ref,
    mask_ref,
    frame_ref,
    near_ref,
    other_ref,
    far_ref,
    sum_ref,
    first_ref,
    second_ref,
    *,
    far_row,
):
    frame = frame_ref[...].reshape(32, 16, 128) * mask_ref[0][None]
    sum_ref[...] = frame.reshape(512, 128)
    coarse = coarse_lanes()
    for r in range(6):
        sum_ref[pl.ds(r, 32, stride=16), :] += near_ref[32 * r : 32 * r + 32]
        sum_ref[pl.ds(8 + r, 32, stride=16), :] += other_ref[32 * r : 32 * r + 32]
    far = far_ref[far_row : far_row + 32]
    for r, shared in enumerate((far, pltpu.roll(far, 128 - FAR_SHIFT, 1))):
        sum_ref[pl.ds(14 + r, 32, stride=16), :] += jnp.where(coarse, shared, 0.0)
    frame = sum_ref[...].reshape(32, 16, 128)
    low, high = edge_lanes(frame, 0), edge_lanes(frame, HI_LANE)
    even = is_even(part_ref)
    first_ref[...] = jnp.where(even, low, high)
    second_ref[...] = jnp.where(even, high, low)


def forward_kernel(
    part_ref,
    shares_ref,
    first_ref,
    second_ref,
    pre_ref,
    cot_ref,
    coarse_ref,
    detail_ref,
    subband_ref,
    analysis_ref,
    synthesis_ref,
    act_ref,
    grad_ref,
    coef_ref,
    frame_ref,
    near_ref,
    other_ref,
    scratch,
    act,
    done,
):
    coef_ref[...] = add_edges(
        shares_ref, is_even(part_ref), first_ref[...], second_ref[...]
    )
    weights = jnp.concatenate(
        [coarse_ref[s].T for s in range(4)] + [detail_ref[s].T for s in range(3)], axis=1
    )
    frame = mixed(coef_ref, weights, subband_ref[...], scratch)
    lon = lon_synthesis(synthesis_ref)
    lat = lat_filters(synthesis_ref, part_ref)
    grads = []
    stores = []
    for q in range(4):
        kernel = dot3(lat, split(synthesis_rows(frame[128 * q : 128 * q + 128], lon)))
        for g in (2 * q, 2 * q + 1):
            channels = slice(4 * g, 4 * g + 4)
            lanes = slice(128 * (g - 2 * q), 128 * (g - 2 * q) + 128)
            pre = kernel[:, lanes] + pre_ref[channels].reshape(256, 128)
            cumulative = 0.5 * (1.0 + lax.erf(pre * math.sqrt(0.5)))
            density = jnp.exp(-0.5 * pre * pre) * (1.0 / math.sqrt(2.0 * math.pi))
            act[channels] = (pre * cumulative).astype(BF16).reshape(4, 64, 128)
            grad = cot_ref[channels].astype(F32).reshape(256, 128) * (cumulative + pre * density)
            grad_ref[channels] = grad.reshape(4, 64, 128)
            grads.append(grad)
        block = pl.ds(8 * q, 8)
        stores.append(pltpu.make_async_copy(act.at[block], act_ref.at[block], done.at[q]))
        stores[q].start()
    frame = analysis(
        jnp.concatenate(grads, axis=1),
        lat_filters(analysis_ref, part_ref),
        lon_analysis(analysis_ref),
    )
    store_frame(frame, frame_ref, near_ref, other_ref)
    for store in stores:
        store.wait()


def weights_kernel(x_ref, g_ref, coef_ref, frame_ref, near_ref, subband_ref, sum_ref):
    def placed(parts, offset):
        row = lax.broadcasted_iota(jnp.int32, (256, 128), 0)
        place = (row // 8 + offset == lane_index((256, 128))).astype(BF16)
        return dot(parts[0], place) + dot(parts[1], place)

    coef = stacked(by_row(coef_ref), subband_ref[...])
    high, low = split(by_row(frame_ref))
    double = dot_nt(jnp.concatenate([high, low], axis=0), coef[0])
    mix = double[:32] + (double[32:] + dot_nt(high, coef[1]))
    mix = jnp.concatenate([mix, jnp.zeros((32, 32), F32)], axis=1)
    field = split(tiled(x_ref[...]))
    grad_pre = split(tiled(g_ref[...]))
    product = jnp.where(same_row((256, 256)), dot3(grad_pre, field, dot_nt), 0.0)
    skip = split(jnp.sum(product.reshape(32, 8, 256), axis=1))
    rows = split(jnp.sum(g_ref[...].reshape(32, 8, 8, 128), axis=1).reshape(256, 128))
    ones = jnp.ones((8, 128), BF16)
    bias = split(dot_nt(ones, rows[0]) + dot_nt(ones, rows[1]))
    sum_ref[0:192] = near_ref[...]
    sum_ref[192:224] = mix[:, :128]
    sum_ref[224:256] = mix[:, 128:] + placed(skip, 96)
    sum_ref[256:264] = placed(bias, 0)


def pair_kernel(own_ref, near_ref, frame_ref, out_ref):
    out_ref[0:72] = own_ref[192:264] + near_ref[192:264]
    out_ref[72:104] = far_rows(frame_ref)


def result_kernel(sum_ref, coarse_ref, detail_ref, skip_ref, bias_ref, cells):
    first = sum_ref[0:32].T
    second = sum_ref[32:64].T
    for s in range(4):
        coarse_ref[s] = first[32 * s : 32 * s + 32] * (1.0 / math.sqrt(cells // 256))
    for s in range(3):
        detail_ref[s] = second[32 * s : 32 * s + 32] * (1.0 / math.sqrt(cells // 64))
    skip_ref[...] = second[96:] * (1.0 / math.sqrt(cells))
    bias_ref[...] = sum_ref[64:65, :32] * (1.0 / math.sqrt(cells))


def skip_back_kernel(g_ref, skip_ref, out_ref):
    product = dot3(expanded(skip_ref[...], dot), split(tiled(g_ref[...])))
    for t in range(8):
        out_ref[:, 8 * t : 8 * t + 8, :] = product[:, 128 * t : 128 * t + 128].reshape(32, 8, 128)


def unmix_kernel(
    part_ref,
    shares_ref,
    first_ref,
    second_ref,
    coarse_ref,
    detail_ref,
    subband_ref,
    synthesis_ref,
    rows_ref,
    whole,
    scratch,
):
    whole[...] = add_edges(shares_ref, is_even(part_ref), first_ref[...], second_ref[...])
    weights = jnp.concatenate(
        [coarse_ref[s] for s in range(4)] + [detail_ref[s] for s in range(3)], axis=1
    )
    frame = mixed(whole, weights, subband_ref[...], scratch)
    rows_ref[...] = synthesis_rows(frame, lon_synthesis(synthesis_ref))


def field_kernel(part_ref, rows_ref, skip_ref, synthesis_ref, out_ref, field, done):
    lat = lat_filters(synthesis_ref, part_ref)
    stores = []
    for q in range(4):
        part = dot3(lat, split(rows_ref[:, 256 * q : 256 * q + 256]))
        for g in (2 * q, 2 * q + 1):
            channels = slice(4 * g, 4 * g + 4)
            lanes = slice(128 * (g - 2 * q), 128 * (g - 2 * q) + 128)
            field[channels] = skip_ref[channels] + part[:, lanes].reshape(4, 64, 128)
        block = pl.ds(8 * q, 8)
        stores.append(pltpu.make_async_copy(field.at[block], out_ref.at[block], done.at[q]))
        stores[q].start()
    for store in stores:
        store.wait()


def full_spec(shape):
    return pl.BlockSpec(shape, lambda *_: (0,) * len(shape))


def part_spec(shape):
    return pl.BlockSpec(shape, lambda _, part: (part[0] // 2,) + (0,) * (len(shape) - 1))


def shape_of(*shape, dtype=F32):
    return jax.ShapeDtypeStruct(shape, dtype)


FRAME = pltpu.VMEM((512, 128), F32)


def call(kernel, outs, args, part=None, by_part=(), scratch=(), in_hbm=()):
    in_specs = [
        part_spec((1,) + arg.shape[1:]) if i in by_part else full_spec(arg.shape)
        for i, arg in enumerate(args)
    ]
    out_specs = [
        pl.BlockSpec(memory_space=pltpu.HBM) if i in in_hbm else full_spec(out.shape)
        for i, out in enumerate(outs)
    ]
    params = pltpu.CompilerParams(vmem_limit_bytes=48 * 1024 * 1024)
    if part is None:
        return pl.pallas_call(
            kernel,
            grid=(1,),
            in_specs=in_specs,
            out_specs=out_specs,
            out_shape=list(outs),
            scratch_shapes=list(scratch),
            compiler_params=params,
        )(*args)
    grid_spec = pltpu.PrefetchScalarGridSpec(
        num_scalar_prefetch=1,
        grid=(1,),
        in_specs=in_specs,
        out_specs=out_specs,
        scratch_shapes=list(scratch),
    )
    return pl.pallas_call(
        kernel, grid_spec=grid_spec, out_shape=list(outs), compiler_params=params
    )(part, *args)


COEFS = shape_of(512, 128)
ROWS = shape_of(192, 128)
FAR = shape_of(32, 128)
EDGE = shape_of(11, 16, 128)
FIELD = shape_of(32, 64, 128)


def swapped(values, axis, distance):
    count = lax.axis_size(axis)
    return lax.ppermute(values, axis, [(i, i ^ distance) for i in range(count)])


def ring(values, unit):
    count = lax.axis_size("lon")
    step = (3, 1, -1, -3)
    return lax.ppermute(
        values, "lon", [(i, i + step[i // unit % 4] * unit) for i in range(count)]
    )


def across(values):
    pairs = []
    for lon in range(lax.axis_size("lon")):
        for lat in range(LAT_PARTS):
            other = lat ^ 2 if lon % 4 in (0, 3) else lat
            pairs.append((LAT_PARTS * lon + lat, LAT_PARTS * (lon ^ 3) + other))
    return lax.ppermute(values, ("lon", "lat"), pairs)


def middle(values):
    return lax.ppermute(values, "lat", [(1, 2), (2, 1)])


def lat_sum(frame, near, other, far, far_row, part):
    return call(
        functools.partial(lat_sum_kernel, far_row=far_row),
        (COEFS, EDGE, EDGE),
        (jnp.asarray(OWN), frame, near, other, far),
        part,
        (0,),
    )


def lon_exchange(first, second):
    count = lax.axis_size("lon")
    pairs = [(i, (i - 1 + 2 * (i % 2)) % count) for i in range(count)]
    return lax.ppermute(first, "lon", pairs), swapped(second, "lon", 1)


def after(values, others):
    return lax.optimization_barrier((values, others))[0]


def on_device(ocean_field, cotangent, mix_coarse, mix_detail, skip_weight, bias_vector):
    part = (2 * lax.axis_index("lat") + lax.axis_index("lon") % 2).astype(jnp.int32).reshape(1)
    analysis_table, synthesis_table = jnp.asarray(ANALYSIS), jnp.asarray(SYNTHESIS)
    subbands = jnp.asarray(SUBBANDS)
    frame, near, other, far = call(
        analysis_kernel,
        (COEFS, ROWS, ROWS, FAR),
        (ocean_field, analysis_table),
        part,
    )
    (pre,) = call(skip_kernel, (FIELD,), (ocean_field, skip_weight, bias_vector.reshape(1, 32)))
    near = swapped(near, "lat", 1)
    other = middle(other)
    far = swapped(far, "lat", 2)
    (near, other, far), pre = lax.optimization_barrier(((near, other, far), pre))
    shares, first, second = lat_sum(frame, near, other, far, 0, part)
    first, second = lon_exchange(first, second)
    activated, grad_pre, coef, frame, near, other = call(
        forward_kernel,
        (shape_of(32, 64, 128, dtype=BF16), FIELD, COEFS, COEFS, ROWS, ROWS),
        (
            shares,
            first,
            second,
            pre,
            cotangent,
            mix_coarse,
            mix_detail,
            subbands,
            analysis_table,
            synthesis_table,
        ),
        part,
        scratch=(FRAME, pltpu.VMEM((32, 64, 128), BF16), pltpu.SemaphoreType.DMA((4,))),
        in_hbm=(0,),
    )
    (own,) = call(
        weights_kernel,
        (shape_of(264, 128),),
        (ocean_field, grad_pre, coef, frame, near, subbands),
    )
    (skip_back,) = call(skip_back_kernel, (FIELD,), (grad_pre, skip_weight))
    near = swapped(own, "lat", 1)
    near, skip_back = lax.optimization_barrier((near, skip_back))
    (pair,) = call(pair_kernel, (shape_of(104, 128),), (own, near, frame))
    far = swapped(pair, "lat", 2)
    other = middle(after(other, near))
    sums = pair[:72] + far[:72]
    steps = [swapped(sums, "lon", k) for k in (4, 12, 8)]
    shares, first, second = lat_sum(frame, near, other, far, 72, part)
    first, second = lon_exchange(first, second)
    sums = sums + steps[0] + (steps[1] + steps[2])
    steps = [swapped(sums, "lon", k) for k in (16, 32)]
    later, second = lax.optimization_barrier((sums, second))
    steps.append(swapped(later, "lon", 48))
    sums = sums + steps[0] + (steps[1] + steps[2])
    (rows,) = call(
        unmix_kernel,
        (shape_of(256, 1024),),
        (shares, first, second, mix_coarse, mix_detail, subbands, synthesis_table),
        part,
        scratch=(FRAME, FRAME),
    )
    sums, rows = lax.optimization_barrier((sums, rows))
    (grad_field,) = call(
        field_kernel,
        (FIELD,),
        (rows, skip_back, synthesis_table),
        part,
        scratch=(pltpu.VMEM((32, 64, 128), F32), pltpu.SemaphoreType.DMA((4,))),
        in_hbm=(0,),
    )
    steps = [swapped(sums, "lon", 1), across(sums), swapped(sums, "lon", 2)]
    sums = sums + steps[0] + (steps[1] + steps[2])
    sums, grad_field = lax.optimization_barrier((sums, grad_field))
    cells = LAT_PARTS * LAT_BLOCK * LON_BLOCK * lax.axis_size("lon")
    coarse, detail, grad_skip, grad_bias = call(
        functools.partial(result_kernel, cells=cells),
        (shape_of(4, 32, 32), shape_of(3, 32, 32), shape_of(32, 32), shape_of(1, 32)),
        (sums,),
    )
    return (activated, grad_field, coarse, detail, grad_skip, grad_bias.reshape(32))


def solution(mesh):
    return jax.shard_map(
        on_device,
        mesh=mesh,
        in_specs=(P(None, "lat", "lon"), P(None, "lat", "lon"), P(), P(), P(), P()),
        out_specs=(P(None, "lat", "lon"), P(None, "lat", "lon"), P(), P(), P(), P()),
        check_vma=False,
    )
```
